32 devices in a mesh: strip: 8 (over z, core), pt: 4 (over y, x).
Axes of the slice: x: 2, y: 2, z: 4, core: 2. Of those that a mesh axis runs over, the one named last changes fastest.
Arguments:
- spectra: float32 [600, 32, 1024], P(None, 'strip', 'pt'), may hold values from 0.01 to 1
- courant: float32 [25], replicated, may hold values from 0.05 to 0.4
- wind_speed: float32 [32, 1024], P('strip', 'pt'), may hold values from 0.5 to 2
- wind_dir: float32 [32, 1024], P('strip', 'pt'), may hold values from -3.140625 to 3.140625
- sea_mask: int32 [32, 1024], P('strip', 'pt'), may hold values 0 or 1
- ice_mask: int32 [32, 1024], P('strip', 'pt'), may hold values 0 or 1
Outputs:
- new_spectra: float32 [600, 32, 1024], P(None, 'strip', 'pt')
The draws below stay inside these ranges and needn't reach their ends.
All inputs are finite; a program needn't handle non-finite values. No bound on the sum of `sea_mask` or of `ice_mask` on one device may be relied on, other than what follows from the above.
Results may differ from the reference program's by a relative error of at most 0.000088.
Values sent between devices are 32-bit elements; how exact they have to be, the bound alone decides.
A program may use at most 64 MiB of HBM per device.

```python
import math
import jax
import jax.numpy as jnp
from jax import lax

NF = 25
ND = 24
SUB = 2
K = 600
NY = 32
NX = 1024


def place_ends(result, own_key, least, high):
    shape = result.shape
    index_at = [jax.random.randint(jax.random.fold_in(own_key, axis), (), 0, shape[axis]) for axis in range(len(shape))]
    result = result.at[tuple(index_at)].set(least)
    longest = shape.index(max(shape))
    index_at[longest] = (index_at[longest] + 1) % shape[longest]
    return result.at[tuple(index_at)].set(high)


def levels(key, shape, pieces, low, largest):
    def one(dim, blocks):
        draws = jax.random.uniform(jax.random.fold_in(jax.random.fold_in(key, 6), dim), (blocks,), jnp.float32, low / len(pieces), largest / len(pieces))
        return jnp.repeat(jnp.exp(draws), shape[dim] // blocks).reshape((-1,) + (1,) * (len(shape) - dim - 1))

    factor_of = one(*pieces[0])
    for cut in pieces[1:]:
        factor_of = factor_of * one(*cut)
    return factor_of


def setup_inputs(seed: int = 0) -> dict:
    key_list = jax.random.split(jax.random.key(seed), 7)
    return {
        "spectra": jnp.clip(jnp.exp(math.log(1.0) - 4.6051702 * jax.random.uniform(key_list[0], (K, NY, NX), jnp.float32) ** levels(key_list[0], (K, NY, NX), ((1, 8), (2, 4)), -0.2, 0.2)), 0.01, 1.0),
        "courant": jnp.clip(jnp.exp(jax.random.uniform(key_list[1], (NF,), jnp.float32, math.log(0.05), math.log(0.4))), 0.05, 0.4),
        "wind_speed": jnp.clip(jnp.exp(math.log(2.0) - 1.3862944 * jax.random.uniform(key_list[2], (NY, NX), jnp.float32) ** levels(key_list[2], (NY, NX), ((0, 8), (1, 4)), -0.2, 0.2)), 0.5, 2.0),
        "wind_dir": jnp.clip(jax.random.uniform(key_list[3], (NY, NX), jnp.float32, -3.140625, 3.140625), -3.140625, 3.140625),
        "sea_mask": place_ends((jax.random.randint(key_list[4], (NY, NX), 0, 4) < 3).astype(jnp.int32), jax.random.fold_in(key_list[4], 1), 0, 1),
        "ice_mask": place_ends((jax.random.randint(key_list[5], (NY, NX), 0, 8) < 1).astype(jnp.int32), jax.random.fold_in(key_list[5], 1), 0, 1),
    }


def tables(courant):
    ratio = 1.1 ** jnp.arange(NF, dtype=jnp.float32)
    theta = 2.0 * jnp.pi * jnp.arange(ND, dtype=jnp.float32) / ND
    speed_u = (courant[:, None] * jnp.cos(theta)[None, :]).reshape(-1)
    speed_v = (courant[:, None] * jnp.sin(theta)[None, :]).reshape(-1)
    return ratio, theta, speed_u, speed_v


def advance(core, west, east, south, north, speed_u, speed_v, sea):
    up_pos = jnp.maximum(speed_u, 0.0)[:, None, None]
    up_neg = jnp.minimum(speed_u, 0.0)[:, None, None]
    vp_pos = jnp.maximum(speed_v, 0.0)[:, None, None]
    vp_neg = jnp.minimum(speed_v, 0.0)[:, None, None]
    fresh = core - up_pos * (core - west) - up_neg * (east - core) - vp_pos * (core - south) - vp_neg * (north - core)
    return fresh * sea


def source(energy, wind_speed, wind_dir, ice_mask, ratio, theta):
    rows = energy.shape[1]
    cols = energy.shape[2]
    field = energy.reshape(NF, ND, rows, cols)
    weight = ratio / (ND * jnp.sum(ratio))
    first = jnp.einsum("fdyx,f->yx", field, weight, precision=lax.Precision.HIGHEST)
    second = jnp.einsum("fdyx,f->yx", field, weight * ratio, precision=lax.Precision.HIGHEST)
    mean_ratio = second / jnp.maximum(first, 0.05)
    icef = ice_mask.astype(jnp.float32)
    align = jnp.maximum(jnp.cos(theta[:, None, None] - wind_dir[None]), 0.0)
    gain = 0.05 * wind_speed[None, None] * ratio[:, None, None, None] * align[None]
    loss = 0.02 * ratio[:, None, None, None] * mean_ratio[None, None]
    net = (1.0 - icef)[None, None] * gain - loss - 0.7 * icef[None, None]
    return (field * jnp.exp(net)).reshape(NF * ND, rows, cols)


def propagate_band(block, speed_u, speed_v, sea):
    for step in range(SUB):
        zero_row = jnp.zeros((block.shape[0], 1, block.shape[2]), jnp.float32)
        south = jnp.concatenate([zero_row, block[:, :-1]], axis=1)
        north = jnp.concatenate([block[:, 1:], zero_row], axis=1)
        west = jnp.roll(block, 1, axis=2)
        east = jnp.roll(block, -1, axis=2)
        block = advance(block, west, east, south, north, speed_u, speed_v, sea[None])
    return block


def reference(spectra, courant, wind_speed, wind_dir, sea_mask, ice_mask):
    ratio, theta, speed_u, speed_v = tables(courant)
    sea = sea_mask.astype(jnp.float32)
    grouped = spectra.reshape(NF, ND, spectra.shape[1], spectra.shape[2])
    moved = lax.map(lambda item: propagate_band(item[0], item[1], item[2], sea),
                    (grouped, speed_u.reshape(NF, ND), speed_v.reshape(NF, ND)))
    energy = moved.reshape(NF * ND, spectra.shape[1], spectra.shape[2])
    by_row = jnp.moveaxis(energy, 1, 0)
    done = lax.map(lambda item: source(item[0][:, None], item[1][None], item[2][None], item[3][None], ratio, theta)[:, 0],
                   (by_row, wind_speed, wind_dir, ice_mask))
    return jnp.moveaxis(done, 0, 1)
```

```python
import functools
import numpy as np
import jax
import jax.numpy as jnp
from jax import lax
from jax.experimental import pallas as pl
from jax.experimental.pallas import tpu as pltpu
from jax.sharding import PartitionSpec as P

NF = 25
ND = 24
HALF = ND // 2
CH = 5
IC = NF // CH
RPI = ND * 8
RPC = RPI * IC
MESH = pl.DeviceIdType.MESH

THETA = (np.float32(2.0 * np.pi) * np.arange(ND, dtype=np.float32) / np.float32(ND)).astype(np.float32)
COS = np.cos(THETA).astype(np.float32)
SIN = np.sin(THETA).astype(np.float32)
RATIO = np.float32(1.1) ** np.arange(NF, dtype=np.float32)
WEIGHT = (RATIO / (ND * np.sum(RATIO, dtype=np.float64))).astype(np.float32)
FROM_WEST = [d for d in range(ND) if COS[d] > 0.0]
FROM_EAST = [d for d in range(ND) if not COS[d] > 0.0]


def pieces():
    return ((0, 0, 8, 0), (0, 8, 4, 8), (1, 0, 4, 12), (1, 4, 8, 16))


def kernel(
    n_strip, n_pt,
    table, courant, wind_speed, wind_dir, sea_mask, ice_mask, spectra,
    out,
    e0, e1, gain, row_send, row_recv, col_send, col_recv,
    in_sem, out_sem, send_sem, recv_sem,
):
    s = lax.axis_index("strip")
    p = lax.axis_index("pt")
    east = lax.rem(p + 1, n_pt)
    west = lax.rem(p + n_pt - 1, n_pt)
    has_south = s > 0
    has_north = s < n_strip - 1

    def load(c):
        rows = pl.ds(pl.multiple_of(c * RPC, RPC), RPC)
        return pltpu.make_async_copy(spectra.at[rows, :], e0.at[rows, :], in_sem.at[c])

    def store(c):
        rows = pl.ds(pl.multiple_of(c * RPC, RPC), RPC)
        return pltpu.make_async_copy(e1.at[rows, :], out.at[rows, :], out_sem.at[c])

    def rows_to(phase, c, way):
        return pltpu.make_async_remote_copy(
            src_ref=row_send.at[phase, c, way],
            dst_ref=row_recv.at[phase, c, way],
            send_sem=send_sem.at[phase, c, way],
            recv_sem=recv_sem.at[phase, c, way],
            device_id={"strip": s + 1 if way == 0 else s - 1},
            device_id_type=MESH,
        )

    def cols_to(phase, c, way):
        return pltpu.make_async_remote_copy(
            src_ref=col_send.at[phase, c],
            dst_ref=col_recv.at[phase, c, way],
            send_sem=send_sem.at[phase, c, 2 + way],
            recv_sem=recv_sem.at[phase, c, 2 + way],
            device_id={"pt": east if way == 0 else west},
            device_id_type=MESH,
        )

    def send(phase, c):
        @pl.when(has_north)
        def _():
            rows_to(phase, c, 0).start()

        @pl.when(has_south)
        def _():
            rows_to(phase, c, 1).start()

        cols_to(phase, c, 0).start()
        cols_to(phase, c, 1).start()

    def receive(phase, c):
        cols_to(phase, c, 0).wait_recv()
        cols_to(phase, c, 1).wait_recv()

        @pl.when(has_south)
        def _():
            rows_to(phase, c, 0).wait_recv()

        @pl.when(has_north)
        def _():
            rows_to(phase, c, 1).wait_recv()

    for c in range(CH):
        load(c).start()

    barrier = pltpu.get_barrier_semaphore()
    for side in (east, west):
        pl.semaphore_signal(barrier, inc=1, device_id={"pt": side}, device_id_type=MESH)

    @pl.when(has_north)
    def _():
        pl.semaphore_signal(barrier, inc=1, device_id={"strip": s + 1}, device_id_type=MESH)

    @pl.when(has_south)
    def _():
        pl.semaphore_signal(barrier, inc=1, device_id={"strip": s - 1}, device_id_type=MESH)

    @pl.when(jnp.logical_not(has_south))
    def _():
        row_recv[:, :, 0] = jnp.zeros(row_recv.shape[:2] + row_recv.shape[3:], jnp.float32)

    @pl.when(jnp.logical_not(has_north))
    def _():
        row_recv[:, :, 1] = jnp.zeros(row_recv.shape[:2] + row_recv.shape[3:], jnp.float32)

    lane = lax.broadcasted_iota(jnp.int32, (8, 128), 1)
    sub = lax.broadcasted_iota(jnp.int32, (8, 128), 0)
    low = sub < 4
    first_lane = lane == 0
    last_lane = lane == 127
    sea = sea_mask[...].astype(jnp.float32)
    ice = ice_mask[...].astype(jnp.float32)

    def pack_rows(src, phase, c):
        def one(il, carry):
            base = pl.multiple_of((c * IC + il) * RPI, 8)
            to = pl.multiple_of(il * ND, 8)
            for tile, first, count, at in pieces():
                up = src[pl.ds(base + first * 8 + 3 + 4 * tile, count, stride=8), :]
                row_send[phase, c, 0, pl.ds(to + at, count), :] = up
                down = src[pl.ds(base + (HALF + first) * 8 + 4 * tile, count, stride=8), :]
                row_send[phase, c, 1, pl.ds(to + at, count), :] = down
            return carry

        lax.fori_loop(0, IC, one, 0)

    def put(acc, m, rolled_pos, neg):
        mixed = jnp.where(low, neg, rolled_pos)
        if m:
            mixed = pltpu.roll(mixed, m, 1)
        return jnp.where(lane == m, mixed, acc)

    pl.semaphore_wait(
        barrier, 2 + has_north.astype(jnp.int32) + has_south.astype(jnp.int32)
    )

    def first_halo(c, carry):
        load(c).wait()
        pack_rows(e0, 0, c)

        def one(il, acc):
            base = pl.multiple_of((c * IC + il) * RPI, 8)
            own = jnp.zeros((8, 128), jnp.float32)
            for m in range(HALF):
                pos = e0[pl.ds(base + 8 * FROM_WEST[m], 8), :]
                neg = e0[pl.ds(base + 8 * FROM_EAST[m], 8), :]
                own = put(own, m, pltpu.roll(pos, 1, 1), neg)
            return jnp.where(lane < HALF, own, pltpu.roll(acc, HALF, 1))

        col_send[0, c] = lax.fori_loop(0, IC, one, jnp.zeros((8, 128), jnp.float32))
        send(0, c)
        return carry

    lax.fori_loop(0, CH, first_halo, 0)

    strength = (1.0 - ice) * 0.05 * wind_speed[...]
    cos_wind = jnp.cos(wind_dir[...])
    sin_wind = jnp.sin(wind_dir[...])
    for d in range(ND):
        align = jnp.maximum(float(COS[d]) * cos_wind + float(SIN[d]) * sin_wind, 0.0)
        gain[pl.ds(8 * d, 8), :] = strength * align

    def advance(src, dst, phase, c, sums):
        receive(phase, c)
        halo = pltpu.roll(jnp.where(low, col_recv[phase, c, 1], col_recv[phase, c, 0]), 4, 0)
        halo = pltpu.roll(halo, 128 - (IC - 1) * HALF, 1)

        def one(il, carry):
            halo, acc, m0, m1 = carry
            i = c * IC + il
            base = pl.multiple_of(i * RPI, 8)
            at = pl.multiple_of(il * ND, 8)
            speed = courant[i] * sea
            keep = [sea - speed * float(k) for k in (np.abs(COS[:4]) + np.abs(SIN[:4]))]
            own = jnp.zeros((8, 128), jnp.float32)
            total = jnp.zeros((8, 128), jnp.float32)

            def step(d, core, side):
                if d < HALF:
                    near = pltpu.roll(core, 1, 0)
                    r0, r1, way, m = 0, 4, 0, d
                else:
                    near = pltpu.roll(core, 7, 0)
                    r0, r1, way, m = 3, 7, 1, d - HALF
                h0 = row_recv[phase, c, way, pl.ds(at + m, 1), :]
                h1 = row_recv[phase, c, way, pl.ds(at + HALF + m, 1), :]
                near = jnp.where(sub == r0, h0, jnp.where(sub == r1, h1, near))
                flow = float(abs(COS[d])) * side + float(abs(SIN[d])) * near
                q = d % 6
                fresh = keep[q if q < 4 else 6 - q] * core + speed * flow
                dst[pl.ds(base + 8 * d, 8), :] = fresh
                return fresh

            for m in range(HALF):
                pos = src[pl.ds(base + 8 * FROM_WEST[m], 8), :]
                neg = src[pl.ds(base + 8 * FROM_EAST[m], 8), :]
                edge = jnp.broadcast_to(halo[:, m : m + 1], (8, 128))
                rolled_pos = pltpu.roll(pos, 1, 1)
                rolled_neg = pltpu.roll(neg, 127, 1)
                swap = pltpu.roll(jnp.where(first_lane, rolled_pos, rolled_neg), 4, 0)
                side_pos = jnp.where(first_lane, jnp.where(low, edge, swap), rolled_pos)
                side_neg = jnp.where(last_lane, jnp.where(low, swap, edge), rolled_neg)
                new_pos = step(FROM_WEST[m], pos, side_pos)
                new_neg = step(FROM_EAST[m], neg, side_neg)
                if phase == 0:
                    own = put(own, m, pltpu.roll(new_pos, 1, 1), new_neg)
                else:
                    total = total + (new_pos + new_neg)
            if phase == 0:
                acc = jnp.where(lane < HALF, own, pltpu.roll(acc, HALF, 1))
            else:
                m0 = m0 + table[1, i] * total
                m1 = m1 + table[2, i] * total
            return pltpu.roll(halo, HALF, 1), acc, m0, m1

        zero = jnp.zeros((8, 128), jnp.float32)
        _, acc, m0, m1 = lax.fori_loop(0, IC, one, (halo, zero) + sums)
        if phase == 0:
            col_send[1, c] = acc
            pack_rows(dst, 1, c)
            send(1, c)
        return m0, m1

    zero = jnp.zeros((8, 128), jnp.float32)

    def first_step(c, carry):
        advance(e0, e1, 0, c, (zero, zero))
        return carry

    lax.fori_loop(0, CH, first_step, 0)
    m0, m1 = lax.fori_loop(
        0, CH, lambda c, sums: advance(e1, e0, 1, c, sums), (zero, zero)
    )
    mean_ratio = m1 / jnp.maximum(m0, 0.05)
    drag = 0.02 * mean_ratio
    cold = 0.7 * ice

    def last(c, carry):
        def one(il, carry):
            i = c * IC + il
            base = pl.multiple_of(i * RPI, 8)
            ratio = table[0, i]
            loss = ratio * drag + cold
            for d in range(ND):
                rows = pl.ds(base + 8 * d, 8)
                e1[rows, :] = e0[rows, :] * jnp.exp(ratio * gain[pl.ds(8 * d, 8), :] - loss)
            return carry

        lax.fori_loop(0, IC, one, 0)
        store(c).start()
        return carry

    lax.fori_loop(0, CH, last, 0)

    def finish(c, carry):
        for phase in range(2):
            @pl.when(has_north)
            def _():
                rows_to(phase, c, 0).wait_send()

            @pl.when(has_south)
            def _():
                rows_to(phase, c, 1).wait_send()

            cols_to(phase, c, 0).wait_send()
            cols_to(phase, c, 1).wait_send()
        store(c).wait()
        return carry

    lax.fori_loop(0, CH, finish, 0)


def to_tiles(x):
    lead, rows, cols = x.shape
    x = x.reshape(lead, rows, cols // 128, 128).transpose(0, 2, 1, 3)
    return x.reshape(lead * rows * cols // 128, 128)


def from_tiles(x, shape):
    lead, rows, cols = shape
    x = x.reshape(lead, cols // 128, rows, 128).transpose(0, 2, 1, 3)
    return x.reshape(shape)


def on_device(n_strip, n_pt, spectra, courant, wind_speed, wind_dir, sea_mask, ice_mask):
    table = jnp.asarray(np.stack([RATIO, WEIGHT, WEIGHT * RATIO]))
    total = spectra.shape[0] * 8
    vmem = pl.BlockSpec(memory_space=pltpu.VMEM)
    smem = pl.BlockSpec(memory_space=pltpu.SMEM)
    hbm = pl.BlockSpec(memory_space=pl.ANY)
    sem = pltpu.SemaphoreType.DMA
    rows = IC * ND
    result = pl.pallas_call(
        functools.partial(kernel, n_strip, n_pt),
        out_shape=jax.ShapeDtypeStruct((total, 128), jnp.float32),
        in_specs=[smem, smem, vmem, vmem, vmem, vmem, hbm],
        out_specs=hbm,
        scratch_shapes=[
            pltpu.VMEM((total, 128), jnp.float32),
            pltpu.VMEM((total, 128), jnp.float32),
            pltpu.VMEM((ND * 8, 128), jnp.float32),
            pltpu.VMEM((2, CH, 2, rows, 128), jnp.float32),
            pltpu.VMEM((2, CH, 2, rows, 128), jnp.float32),
            pltpu.VMEM((2, CH, 8, 128), jnp.float32),
            pltpu.VMEM((2, CH, 2, 8, 128), jnp.float32),
            sem((CH,)),
            sem((CH,)),
            sem((2, CH, 4)),
            sem((2, CH, 4)),
        ],
        compiler_params=pltpu.CompilerParams(
            collective_id=0, has_side_effects=True, vmem_limit_bytes=32 * 1024 * 1024
        ),
        cost_estimate=pl.CostEstimate(
            flops=40 * total * 128, bytes_accessed=8 * total * 128, transcendentals=total * 128
        ),
    )(
        table,
        courant,
        to_tiles(wind_speed[None]),
        to_tiles(wind_dir[None]),
        to_tiles(sea_mask[None]),
        to_tiles(ice_mask[None]),
        to_tiles(spectra),
    )
    return from_tiles(result, spectra.shape)


def solution(mesh):
    in_specs = (
        P(None, "strip", "pt"),
        P(),
        P("strip", "pt"),
        P("strip", "pt"),
        P("strip", "pt"),
        P("strip", "pt"),
    )
    return jax.shard_map(
        functools.partial(on_device, mesh.shape["strip"], mesh.shape["pt"]),
        mesh=mesh,
        in_specs=in_specs,
        out_specs=P(None, "strip", "pt"),
        check_vma=False,
    )
```

```python
import functools
import numpy as np
import jax
import jax.numpy as jnp
from jax import lax
from jax.experimental import pallas as pl
from jax.experimental.pallas import tpu as pltpu
from jax.sharding import PartitionSpec as P

NF = 25
ND = 24
HALF = ND // 2
CH = 5
IC = NF // CH
RPI = ND * 8
RPC = RPI * IC
MESH = pl.DeviceIdType.MESH

THETA = (np.float32(2.0 * np.pi) * np.arange(ND, dtype=np.float32) / np.float32(ND)).astype(np.float32)
COS = np.cos(THETA).astype(np.float32)
SIN = np.sin(THETA).astype(np.float32)
RATIO = np.float32(1.1) ** np.arange(NF, dtype=np.float32)
WEIGHT = (RATIO / (ND * np.sum(RATIO, dtype=np.float64))).astype(np.float32)
FROM_WEST = [d for d in range(ND) if COS[d] > 0.0]
FROM_EAST = [d for d in range(ND) if not COS[d] > 0.0]


def pieces():
    return ((0, 0, 8, 0), (0, 8, 4, 8), (1, 0, 4, 12), (1, 4, 8, 16))


def kernel(
    n_strip, n_pt,
    courant_in, sea_in, spectra,
    out, mean_ratio,
    e0, e1, sea_mask, courant, table,
    row_send, row_recv, col_send, col_recv,
    in_sem, out_sem, small_sem, send_sem, recv_sem,
):
    s = lax.axis_index("strip")
    p = lax.axis_index("pt")
    east = lax.rem(p + 1, n_pt)
    west = lax.rem(p + n_pt - 1, n_pt)
    has_south = s > 0
    has_north = s < n_strip - 1

    def load(c):
        rows = pl.ds(pl.multiple_of(c * RPC, RPC), RPC)
        return pltpu.make_async_copy(spectra.at[rows, :], e0.at[rows, :], in_sem.at[c])

    def store(c):
        rows = pl.ds(pl.multiple_of(c * RPC, RPC), RPC)
        return pltpu.make_async_copy(e0.at[rows, :], out.at[rows, :], out_sem.at[c])

    def rows_to(phase, c, way):
        return pltpu.make_async_remote_copy(
            src_ref=row_send.at[phase, c, way],
            dst_ref=row_recv.at[phase, c, way],
            send_sem=send_sem.at[phase, c, way],
            recv_sem=recv_sem.at[phase, c, way],
            device_id={"strip": s + 1 if way == 0 else s - 1},
            device_id_type=MESH,
        )

    def cols_to(phase, c, way):
        return pltpu.make_async_remote_copy(
            src_ref=col_send.at[phase, c],
            dst_ref=col_recv.at[phase, c, way],
            send_sem=send_sem.at[phase, c, 2 + way],
            recv_sem=recv_sem.at[phase, c, 2 + way],
            device_id={"pt": east if way == 0 else west},
            device_id_type=MESH,
        )

    def send(phase, c):
        @pl.when(has_north)
        def _():
            rows_to(phase, c, 0).start()

        @pl.when(has_south)
        def _():
            rows_to(phase, c, 1).start()

        cols_to(phase, c, 0).start()
        cols_to(phase, c, 1).start()

    def receive(phase, c):
        cols_to(phase, c, 0).wait_recv()
        cols_to(phase, c, 1).wait_recv()

        @pl.when(has_south)
        def _():
            rows_to(phase, c, 0).wait_recv()

        @pl.when(has_north)
        def _():
            rows_to(phase, c, 1).wait_recv()

    smalls = [
        pltpu.make_async_copy(source, target, small_sem.at[n])
        for n, (source, target) in enumerate(
            ((courant_in, courant), (sea_in, sea_mask))
        )
    ]
    for c in range(CH):
        load(c).start()
    for small in smalls:
        small.start()
    for i in range(NF):
        table[0, i] = float(WEIGHT[i])
        table[1, i] = float(WEIGHT[i] * RATIO[i])

    barrier = pltpu.get_barrier_semaphore()
    for side in (east, west):
        pl.semaphore_signal(barrier, inc=1, device_id={"pt": side}, device_id_type=MESH)

    @pl.when(has_north)
    def _():
        pl.semaphore_signal(barrier, inc=1, device_id={"strip": s + 1}, device_id_type=MESH)

    @pl.when(has_south)
    def _():
        pl.semaphore_signal(barrier, inc=1, device_id={"strip": s - 1}, device_id_type=MESH)

    @pl.when(jnp.logical_not(has_south))
    def _():
        row_recv[:, :, 0] = jnp.zeros(row_recv.shape[:2] + row_recv.shape[3:], jnp.float32)

    @pl.when(jnp.logical_not(has_north))
    def _():
        row_recv[:, :, 1] = jnp.zeros(row_recv.shape[:2] + row_recv.shape[3:], jnp.float32)

    lane = lax.broadcasted_iota(jnp.int32, (8, 128), 1)
    sub = lax.broadcasted_iota(jnp.int32, (8, 128), 0)
    low = sub < 4
    first_lane = lane == 0
    last_lane = lane == 127

    def pack_rows(src, phase, c):
        def one(il, carry):
            base = pl.multiple_of((c * IC + il) * RPI, 8)
            to = pl.multiple_of(il * ND, 8)
            for tile, first, count, at in pieces():
                up = src[pl.ds(base + first * 8 + 3 + 4 * tile, count, stride=8), :]
                row_send[phase, c, 0, pl.ds(to + at, count), :] = up
                down = src[pl.ds(base + (HALF + first) * 8 + 4 * tile, count, stride=8), :]
                row_send[phase, c, 1, pl.ds(to + at, count), :] = down
            return carry

        lax.fori_loop(0, IC, one, 0, unroll=True)

    def put(acc, m, rolled_pos, neg):
        mixed = jnp.where(low, neg, rolled_pos)
        if m:
            mixed = pltpu.roll(mixed, m, 1)
        return jnp.where(lane == m, mixed, acc)

    pl.semaphore_wait(
        barrier, 2 + has_north.astype(jnp.int32) + has_south.astype(jnp.int32)
    )

    def first_halo(c, carry):
        load(c).wait()
        pack_rows(e0, 0, c)

        def one(il, acc):
            base = pl.multiple_of((c * IC + il) * RPI, 8)
            own = jnp.zeros((8, 128), jnp.float32)
            for m in range(HALF):
                pos = e0[pl.ds(base + 8 * FROM_WEST[m], 8), :]
                neg = e0[pl.ds(base + 8 * FROM_EAST[m], 8), :]
                own = put(own, m, pltpu.roll(pos, 1, 1), neg)
            return jnp.where(lane < HALF, own, pltpu.roll(acc, HALF, 1))

        col_send[0, c] = lax.fori_loop(
            0, IC, one, jnp.zeros((8, 128), jnp.float32), unroll=True
        )
        send(0, c)
        return carry

    lax.fori_loop(0, CH, first_halo, 0)

    for small in smalls:
        small.wait()
    sea = sea_mask[...].astype(jnp.float32)

    def advance(src, dst, phase, c, sums):
        receive(phase, c)
        halo = pltpu.roll(jnp.where(low, col_recv[phase, c, 1], col_recv[phase, c, 0]), 4, 0)
        halo = pltpu.roll(halo, 128 - (IC - 1) * HALF, 1)

        def one(il, carry):
            halo, acc, m0, m1 = carry
            i = c * IC + il
            base = pl.multiple_of(i * RPI, 8)
            at = pl.multiple_of(il * ND, 8)
            speed = courant[i] * sea
            keep = [sea - speed * float(k) for k in (np.abs(COS[:4]) + np.abs(SIN[:4]))]
            own = jnp.zeros((8, 128), jnp.float32)
            total = jnp.zeros((8, 128), jnp.float32)

            def step(d, core, side):
                if d < HALF:
                    near = pltpu.roll(core, 1, 0)
                    r0, r1, way, m = 0, 4, 0, d
                else:
                    near = pltpu.roll(core, 7, 0)
                    r0, r1, way, m = 3, 7, 1, d - HALF
                h0 = row_recv[phase, c, way, pl.ds(at + m, 1), :]
                h1 = row_recv[phase, c, way, pl.ds(at + HALF + m, 1), :]
                near = jnp.where(sub == r0, h0, jnp.where(sub == r1, h1, near))
                flow = float(abs(COS[d])) * side + float(abs(SIN[d])) * near
                q = d % 6
                fresh = keep[q if q < 4 else 6 - q] * core + speed * flow
                dst[pl.ds(base + 8 * d, 8), :] = fresh
                return fresh

            for m in range(HALF):
                pos = src[pl.ds(base + 8 * FROM_WEST[m], 8), :]
                neg = src[pl.ds(base + 8 * FROM_EAST[m], 8), :]
                edge = jnp.broadcast_to(halo[:, m : m + 1], (8, 128))
                rolled_pos = pltpu.roll(pos, 1, 1)
                rolled_neg = pltpu.roll(neg, 127, 1)
                swap = pltpu.roll(jnp.where(first_lane, rolled_pos, rolled_neg), 4, 0)
                side_pos = jnp.where(first_lane, jnp.where(low, edge, swap), rolled_pos)
                side_neg = jnp.where(last_lane, jnp.where(low, swap, edge), rolled_neg)
                new_pos = step(FROM_WEST[m], pos, side_pos)
                new_neg = step(FROM_EAST[m], neg, side_neg)
                if phase == 0:
                    own = put(own, m, pltpu.roll(new_pos, 1, 1), new_neg)
                else:
                    total = total + (new_pos + new_neg)
            if phase == 0:
                acc = jnp.where(lane < HALF, own, pltpu.roll(acc, HALF, 1))
            else:
                m0 = m0 + table[0, i] * total
                m1 = m1 + table[1, i] * total
            return pltpu.roll(halo, HALF, 1), acc, m0, m1

        zero = jnp.zeros((8, 128), jnp.float32)
        _, acc, m0, m1 = lax.fori_loop(0, IC, one, (halo, zero) + sums, unroll=True)
        if phase == 0:
            col_send[1, c] = acc
            pack_rows(dst, 1, c)
            send(1, c)
        return m0, m1

    zero = jnp.zeros((8, 128), jnp.float32)

    def first_step(c, carry):
        advance(e0, e1, 0, c, (zero, zero))
        return carry

    lax.fori_loop(0, CH, first_step, 0)
    def second_step(c, sums):
        sums = advance(e1, e0, 1, c, sums)
        store(c).start()
        return sums

    m0, m1 = lax.fori_loop(0, CH, second_step, (zero, zero))
    mean_ratio[...] = m1 / jnp.maximum(m0, 0.05)

    def finish(c, carry):
        for phase in range(2):
            @pl.when(has_north)
            def _():
                rows_to(phase, c, 0).wait_send()

            @pl.when(has_south)
            def _():
                rows_to(phase, c, 1).wait_send()

            cols_to(phase, c, 0).wait_send()
            cols_to(phase, c, 1).wait_send()
        store(c).wait()
        return carry

    lax.fori_loop(0, CH, finish, 0)


def source_kernel(
    wind_speed_in, wind_dir_in, ice_in, mean_ratio_in, energy,
    out,
    held, done, wind_speed, wind_dir, ice_mask, mean_ratio, gain,
    in_sem, out_sem, small_sem,
):
    loads = [
        pltpu.make_async_copy(
            energy.at[pl.ds(c * RPC, RPC), :], held.at[pl.ds(c * RPC, RPC), :], in_sem.at[c]
        )
        for c in range(CH)
    ]
    stores = [
        pltpu.make_async_copy(
            done.at[pl.ds(c * RPC, RPC), :], out.at[pl.ds(c * RPC, RPC), :], out_sem.at[c]
        )
        for c in range(CH)
    ]
    smalls = [
        pltpu.make_async_copy(source, target, small_sem.at[n])
        for n, (source, target) in enumerate(
            (
                (wind_dir_in, wind_dir),
                (wind_speed_in, wind_speed),
                (ice_in, ice_mask),
                (mean_ratio_in, mean_ratio),
            )
        )
    ]
    for copy in smalls + loads:
        copy.start()
    for copy in smalls:
        copy.wait()
    ice = ice_mask[...].astype(jnp.float32)
    strength = (1.0 - ice) * 0.05 * wind_speed[...]
    cos_wind = strength * jnp.cos(wind_dir[...])
    sin_wind = strength * jnp.sin(wind_dir[...])
    for d in range(ND):
        gain[pl.ds(8 * d, 8), :] = jnp.maximum(
            float(COS[d]) * cos_wind + float(SIN[d]) * sin_wind, 0.0
        )
    drag = 0.02 * mean_ratio[...]
    cold = 0.7 * ice
    for c in range(CH):
        loads[c].wait()
        losses = [float(RATIO[c * IC + il]) * drag + cold for il in range(IC)]

        def one(d, carry):
            push = gain[pl.ds(pl.multiple_of(8 * d, 8), 8), :]
            for il in range(IC):
                rows = pl.ds(pl.multiple_of((c * IC + il) * RPI + 8 * d, 8), 8)
                net = float(RATIO[c * IC + il]) * push - losses[il]
                done[rows, :] = held[rows, :] * jnp.exp(net)
            return carry

        lax.fori_loop(0, ND, one, 0, unroll=8)
        stores[c].start()
    for copy in stores:
        copy.wait()


def to_tiles(x):
    lead, rows, cols = x.shape
    x = x.reshape(lead, rows, cols // 128, 128).transpose(0, 2, 1, 3)
    return x.reshape(lead * rows * cols // 128, 128)


def from_tiles(x, shape):
    lead, rows, cols = shape
    x = x.reshape(lead, cols // 128, rows, 128).transpose(0, 2, 1, 3)
    return x.reshape(shape)


def on_device(n_strip, n_pt, spectra, courant, wind_speed, wind_dir, sea_mask, ice_mask):
    total = spectra.shape[0] * 8
    vmem = pl.BlockSpec(memory_space=pltpu.VMEM)
    hbm = pl.BlockSpec(memory_space=pl.ANY)
    sem = pltpu.SemaphoreType.DMA
    rows = IC * ND
    whole = jax.ShapeDtypeStruct((total, 128), jnp.float32)
    point = jax.ShapeDtypeStruct((8, 128), jnp.float32)
    energy, mean_ratio = pl.pallas_call(
        functools.partial(kernel, n_strip, n_pt),
        out_shape=[whole, point],
        in_specs=[hbm] * 3,
        out_specs=[hbm, vmem],
        scratch_shapes=[
            pltpu.VMEM((total, 128), jnp.float32),
            pltpu.VMEM((total, 128), jnp.float32),
            pltpu.VMEM((8, 128), jnp.int32),
            pltpu.SMEM((NF,), jnp.float32),
            pltpu.SMEM((2, NF), jnp.float32),
            pltpu.VMEM((2, CH, 2, rows, 128), jnp.float32),
            pltpu.VMEM((2, CH, 2, rows, 128), jnp.float32),
            pltpu.VMEM((2, CH, 8, 128), jnp.float32),
            pltpu.VMEM((2, CH, 2, 8, 128), jnp.float32),
            sem((CH,)),
            sem((CH,)),
            sem((2,)),
            sem((2, CH, 4)),
            sem((2, CH, 4)),
        ],
        compiler_params=pltpu.CompilerParams(
            collective_id=0, has_side_effects=True, vmem_limit_bytes=60 * 1024 * 1024
        ),
        cost_estimate=pl.CostEstimate(
            flops=30 * total * 128, bytes_accessed=8 * total * 128, transcendentals=0
        ),
    )(courant, to_tiles(sea_mask[None]), to_tiles(spectra))
    result = pl.pallas_call(
        source_kernel,
        out_shape=whole,
        in_specs=[hbm] * 5,
        out_specs=hbm,
        scratch_shapes=[
            pltpu.VMEM((total, 128), jnp.float32),
            pltpu.VMEM((total, 128), jnp.float32),
            pltpu.VMEM((8, 128), jnp.float32),
            pltpu.VMEM((8, 128), jnp.float32),
            pltpu.VMEM((8, 128), jnp.int32),
            pltpu.VMEM((8, 128), jnp.float32),
            pltpu.VMEM((ND * 8, 128), jnp.float32),
            sem((CH,)),
            sem((CH,)),
            sem((4,)),
        ],
        compiler_params=pltpu.CompilerParams(vmem_limit_bytes=60 * 1024 * 1024),
        cost_estimate=pl.CostEstimate(
            flops=4 * total * 128, bytes_accessed=8 * total * 128, transcendentals=total * 128
        ),
    )(
        to_tiles(wind_speed[None]),
        to_tiles(wind_dir[None]),
        to_tiles(ice_mask[None]),
        mean_ratio,
        energy,
    )
    return from_tiles(result, spectra.shape)


def solution(mesh):
    in_specs = (
        P(None, "strip", "pt"),
        P(),
        P("strip", "pt"),
        P("strip", "pt"),
        P("strip", "pt"),
        P("strip", "pt"),
    )
    return jax.shard_map(
        functools.partial(on_device, mesh.shape["strip"], mesh.shape["pt"]),
        mesh=mesh,
        in_specs=in_specs,
        out_specs=P(None, "strip", "pt"),
        check_vma=False,
    )
```

```python
import functools
import numpy as np
import jax
import jax.numpy as jnp
from jax import lax
from jax.experimental import pallas as pl
from jax.experimental.pallas import tpu as pltpu
from jax.sharding import PartitionSpec as P

NF = 25
ND = 24
HALF = ND // 2
CH = 5
IC = NF // CH
RPI = ND * 8
RPC = RPI * IC
MESH = pl.DeviceIdType.MESH

THETA = (np.float32(2.0 * np.pi) * np.arange(ND, dtype=np.float32) / np.float32(ND)).astype(np.float32)
COS = np.cos(THETA).astype(np.float32)
SIN = np.sin(THETA).astype(np.float32)
RATIO = np.float32(1.1) ** np.arange(NF, dtype=np.float32)
WEIGHT = (RATIO / (ND * np.sum(RATIO, dtype=np.float64))).astype(np.float32)
FROM_WEST = [d for d in range(ND) if COS[d] > 0.0]
FROM_EAST = [d for d in range(ND) if not COS[d] > 0.0]


def pieces():
    return ((0, 0, 8, 0), (0, 8, 4, 8), (1, 0, 4, 12), (1, 4, 8, 16))


def kernel(
    n_strip, n_pt,
    courant_in, sea_in, spectra,
    out, mean_ratio,
    e0, e1, sea_mask, sea, courant, table, rise,
    row_send, row_recv, col_send, col_recv,
    in_sem, out_sem, small_sem, send_sem, recv_sem,
):
    s = lax.axis_index("strip")
    p = lax.axis_index("pt")
    east = lax.rem(p + 1, n_pt)
    west = lax.rem(p + n_pt - 1, n_pt)
    has_south = s > 0
    has_north = s < n_strip - 1

    def load(c):
        rows = pl.ds(pl.multiple_of(c * RPC, RPC), RPC)
        return pltpu.make_async_copy(spectra.at[rows, :], e0.at[rows, :], in_sem.at[c])

    def store(c):
        rows = pl.ds(pl.multiple_of(c * RPC, RPC), RPC)
        return pltpu.make_async_copy(e0.at[rows, :], out.at[rows, :], out_sem.at[c])

    def rows_to(phase, c, way):
        return pltpu.make_async_remote_copy(
            src_ref=row_send.at[phase, c, way],
            dst_ref=row_recv.at[phase, c, way],
            send_sem=send_sem.at[phase, c, way],
            recv_sem=recv_sem.at[phase, c, way],
            device_id={"strip": s + 1 if way == 0 else s - 1},
            device_id_type=MESH,
        )

    def cols_to(phase, c, way):
        return pltpu.make_async_remote_copy(
            src_ref=col_send.at[phase, c],
            dst_ref=col_recv.at[phase, c, way],
            send_sem=send_sem.at[phase, c, 2 + way],
            recv_sem=recv_sem.at[phase, c, 2 + way],
            device_id={"pt": east if way == 0 else west},
            device_id_type=MESH,
        )

    def send_rows(phase, c):
        @pl.when(has_north)
        def _():
            rows_to(phase, c, 0).start()

        @pl.when(has_south)
        def _():
            rows_to(phase, c, 1).start()

    def send_cols(phase, c):
        cols_to(phase, c, 0).start()
        cols_to(phase, c, 1).start()

    def receive_rows(phase, c):
        @pl.when(has_south)
        def _():
            rows_to(phase, c, 0).wait_recv()

        @pl.when(has_north)
        def _():
            rows_to(phase, c, 1).wait_recv()

    def receive_cols(phase, c):
        cols_to(phase, c, 0).wait_recv()
        cols_to(phase, c, 1).wait_recv()

    smalls = [
        pltpu.make_async_copy(source, target, small_sem.at[n])
        for n, (source, target) in enumerate(
            ((courant_in, courant), (sea_in, sea_mask))
        )
    ]
    for c in range(CH):
        load(c).start()
    for small in smalls:
        small.start()

    barrier = pltpu.get_barrier_semaphore()
    for side in (east, west):
        pl.semaphore_signal(barrier, inc=1, device_id={"pt": side}, device_id_type=MESH)

    @pl.when(has_north)
    def _():
        pl.semaphore_signal(barrier, inc=1, device_id={"strip": s + 1}, device_id_type=MESH)

    @pl.when(has_south)
    def _():
        pl.semaphore_signal(barrier, inc=1, device_id={"strip": s - 1}, device_id_type=MESH)

    @pl.when(jnp.logical_not(has_south))
    def _():
        row_recv[:, :, 0] = jnp.zeros(row_recv.shape[:2] + row_recv.shape[3:], jnp.float32)

    @pl.when(jnp.logical_not(has_north))
    def _():
        row_recv[:, :, 1] = jnp.zeros(row_recv.shape[:2] + row_recv.shape[3:], jnp.float32)

    for i in range(NF):
        table[0, i] = float(WEIGHT[i])
        table[1, i] = float(WEIGHT[i] * RATIO[i])
    for d in range(HALF):
        rise[pl.ds(d, 1), :] = jnp.full((1, 128), float(abs(SIN[d])), jnp.float32)
        rise[pl.ds(16 + d, 1), :] = jnp.full((1, 128), float(abs(SIN[HALF + d])), jnp.float32)
    lane = lax.broadcasted_iota(jnp.int32, (8, 128), 1)
    sub = lax.broadcasted_iota(jnp.int32, (8, 128), 0)
    low = sub < 4
    first_lane = lane == 0
    last_lane = lane == 127

    def pack_rows(src, phase, c):
        def one(il, carry):
            base = pl.multiple_of((c * IC + il) * RPI, 8)
            to = pl.multiple_of(il * ND, 8)
            for tile, first, count, at in pieces():
                up = src[pl.ds(base + first * 8 + 3 + 4 * tile, count, stride=8), :]
                row_send[phase, c, 0, pl.ds(to + at, count), :] = up
                down = src[pl.ds(base + (HALF + first) * 8 + 4 * tile, count, stride=8), :]
                row_send[phase, c, 1, pl.ds(to + at, count), :] = down
            return carry

        lax.fori_loop(0, IC, one, 0, unroll=True)

    def put(acc, m, rolled_pos, neg):
        mixed = jnp.where(low, neg, rolled_pos)
        if m:
            mixed = pltpu.roll(mixed, m, 1)
        return jnp.where(lane == m, mixed, acc)

    def pack_cols(src, phase, c):
        def one(il, acc):
            base = pl.multiple_of((c * IC + il) * RPI, 8)
            own = jnp.zeros((8, 128), jnp.float32)
            for m in range(HALF):
                pos = src[pl.ds(base + 8 * FROM_WEST[m], 8), :]
                neg = src[pl.ds(base + 8 * FROM_EAST[m], 8), :]
                own = put(own, m, pltpu.roll(pos, 1, 1), neg)
            return jnp.where(lane < HALF, own, pltpu.roll(acc, HALF, 1))

        col_send[phase, c] = lax.fori_loop(
            0, IC, one, jnp.zeros((8, 128), jnp.float32), unroll=True
        )

    load(0).wait()
    pack_cols(e0, 0, 0)
    pack_rows(e0, 0, 0)
    pl.semaphore_wait(
        barrier, 2 + has_north.astype(jnp.int32) + has_south.astype(jnp.int32)
    )
    send_cols(0, 0)
    send_rows(0, 0)

    def first_halo(c, carry):
        load(c).wait()
        pack_cols(e0, 0, c)
        send_cols(0, c)
        pack_rows(e0, 0, c)
        send_rows(0, c)
        return carry

    lax.fori_loop(1, CH, first_halo, 0)
    for small in smalls:
        small.wait()
    sea[...] = sea_mask[...].astype(jnp.float32)

    def advance(src, dst, phase, c, sums):
        receive_cols(phase, c)
        if phase == 1:
            receive_rows(phase, c)
        halo = pltpu.roll(jnp.where(low, col_recv[phase, c, 1], col_recv[phase, c, 0]), 4, 0)
        halo = pltpu.roll(halo, 128 - (IC - 1) * HALF, 1)
        sea_now = sea[...]

        def one(il, carry):
            halo, m0, m1 = carry
            i = c * IC + il
            base = pl.multiple_of(i * RPI, 8)
            at = pl.multiple_of(il * ND, 8)
            speed = courant[i] * sea_now
            keep = [sea_now - speed * float(k) for k in (np.abs(COS[:4]) + np.abs(SIN[:4]))]
            total = jnp.zeros((8, 128), jnp.float32)

            def step(d, core, side):
                if d < HALF:
                    near = pltpu.roll(core, 1, 0)
                    r0, r1, way, m = 0, 4, 0, d
                else:
                    near = pltpu.roll(core, 7, 0)
                    r0, r1, way, m = 3, 7, 1, d - HALF
                if phase == 0:
                    near = jnp.where((sub == r0) | (sub == r1), 0.0, near)
                else:
                    h0 = row_recv[phase, c, way, pl.ds(at + m, 1), :]
                    h1 = row_recv[phase, c, way, pl.ds(at + HALF + m, 1), :]
                    near = jnp.where(sub == r0, h0, jnp.where(sub == r1, h1, near))
                flow = float(abs(COS[d])) * side + float(abs(SIN[d])) * near
                q = d % 6
                fresh = keep[q if q < 4 else 6 - q] * core + speed * flow
                dst[pl.ds(base + 8 * d, 8), :] = fresh
                return fresh

            for m in range(HALF):
                pos = src[pl.ds(base + 8 * FROM_WEST[m], 8), :]
                neg = src[pl.ds(base + 8 * FROM_EAST[m], 8), :]
                edge = jnp.broadcast_to(halo[:, m : m + 1], (8, 128))
                rolled_pos = pltpu.roll(pos, 1, 1)
                rolled_neg = pltpu.roll(neg, 127, 1)
                swap = pltpu.roll(jnp.where(first_lane, rolled_pos, rolled_neg), 4, 0)
                side_pos = jnp.where(first_lane, jnp.where(low, edge, swap), rolled_pos)
                side_neg = jnp.where(last_lane, jnp.where(low, swap, edge), rolled_neg)
                new_pos = step(FROM_WEST[m], pos, side_pos)
                new_neg = step(FROM_EAST[m], neg, side_neg)
                if phase == 1:
                    total = total + (new_pos + new_neg)
            if phase == 1:
                m0 = m0 + table[0, i] * total
                m1 = m1 + table[1, i] * total
            return pltpu.roll(halo, HALF, 1), m0, m1

        _, m0, m1 = lax.fori_loop(0, IC, one, (halo,) + sums, unroll=True)
        return m0, m1

    zero = jnp.zeros((8, 128), jnp.float32)

    def first_step(c, carry):
        advance(e0, e1, 0, c, (zero, zero))
        pack_rows(e1, 1, c)
        send_rows(1, c)
        return carry

    lax.fori_loop(0, CH, first_step, 0)

    def first_edge(c, carry):
        receive_rows(0, c)

        def one(il, carry):
            i = c * IC + il
            base = pl.multiple_of(i * RPI, 8)
            at = pl.multiple_of(il * ND, 8)
            for way in range(2):
                for tile, first, count, to in pieces():
                    row = 4 * tile + 3 * way
                    rows = pl.ds(base + (HALF * way + first) * 8 + row, count, stride=8)
                    speed = courant[i] * sea[pl.ds(row, 1), :]
                    term = row_recv[0, c, way, pl.ds(at + to, count), :]
                    term = term * rise[pl.ds(16 * way + first, count), :]
                    e1[rows, :] = e1[rows, :] + speed * term
            return carry

        lax.fori_loop(0, IC, one, 0, unroll=True)
        pack_cols(e1, 1, c)
        send_cols(1, c)
        return carry

    lax.fori_loop(0, CH, first_edge, 0)

    def second_step(c, sums):
        sums = advance(e1, e0, 1, c, sums)
        store(c).start()
        return sums

    m0, m1 = lax.fori_loop(0, CH, second_step, (zero, zero))
    mean_ratio[...] = m1 / jnp.maximum(m0, 0.05)

    def finish(c, carry):
        for phase in range(2):
            @pl.when(has_north)
            def _():
                rows_to(phase, c, 0).wait_send()

            @pl.when(has_south)
            def _():
                rows_to(phase, c, 1).wait_send()

            cols_to(phase, c, 0).wait_send()
            cols_to(phase, c, 1).wait_send()
        store(c).wait()
        return carry

    lax.fori_loop(0, CH, finish, 0)


def source_kernel(
    wind_speed_in, wind_dir_in, ice_in, mean_ratio_in, energy,
    out,
    held, done, wind_speed, wind_dir, ice_mask, mean_ratio, gain,
    in_sem, out_sem, small_sem,
):
    loads = [
        pltpu.make_async_copy(
            energy.at[pl.ds(c * RPC, RPC), :], held.at[pl.ds(c * RPC, RPC), :], in_sem.at[c]
        )
        for c in range(CH)
    ]
    stores = [
        pltpu.make_async_copy(
            done.at[pl.ds(c * RPC, RPC), :], out.at[pl.ds(c * RPC, RPC), :], out_sem.at[c]
        )
        for c in range(CH)
    ]
    smalls = [
        pltpu.make_async_copy(source, target, small_sem.at[n])
        for n, (source, target) in enumerate(
            (
                (wind_dir_in, wind_dir),
                (wind_speed_in, wind_speed),
                (ice_in, ice_mask),
                (mean_ratio_in, mean_ratio),
            )
        )
    ]
    for copy in smalls + loads:
        copy.start()
    for copy in smalls:
        copy.wait()
    ice = ice_mask[...].astype(jnp.float32)
    strength = (1.0 - ice) * 0.05 * wind_speed[...]
    cos_wind = strength * jnp.cos(wind_dir[...])
    sin_wind = strength * jnp.sin(wind_dir[...])
    for d in range(ND):
        gain[pl.ds(8 * d, 8), :] = jnp.maximum(
            float(COS[d]) * cos_wind + float(SIN[d]) * sin_wind, 0.0
        )
    drag = 0.02 * mean_ratio[...]
    cold = 0.7 * ice
    for c in range(CH):
        loads[c].wait()
        losses = [float(RATIO[c * IC + il]) * drag + cold for il in range(IC)]

        def one(d, carry):
            push = gain[pl.ds(pl.multiple_of(8 * d, 8), 8), :]
            for il in range(IC):
                rows = pl.ds(pl.multiple_of((c * IC + il) * RPI + 8 * d, 8), 8)
                net = float(RATIO[c * IC + il]) * push - losses[il]
                done[rows, :] = held[rows, :] * jnp.exp(net)
            return carry

        lax.fori_loop(0, ND, one, 0, unroll=8)
        stores[c].start()
    for copy in stores:
        copy.wait()


def to_tiles(x):
    lead, rows, cols = x.shape
    x = x.reshape(lead, rows, cols // 128, 128).transpose(0, 2, 1, 3)
    return x.reshape(lead * rows * cols // 128, 128)


def from_tiles(x, shape):
    lead, rows, cols = shape
    x = x.reshape(lead, cols // 128, rows, 128).transpose(0, 2, 1, 3)
    return x.reshape(shape)


def on_device(n_strip, n_pt, spectra, courant, wind_speed, wind_dir, sea_mask, ice_mask):
    total = spectra.shape[0] * 8
    vmem = pl.BlockSpec(memory_space=pltpu.VMEM)
    hbm = pl.BlockSpec(memory_space=pl.ANY)
    sem = pltpu.SemaphoreType.DMA
    rows = IC * ND
    whole = jax.ShapeDtypeStruct((total, 128), jnp.float32)
    point = jax.ShapeDtypeStruct((8, 128), jnp.float32)
    energy, mean_ratio = pl.pallas_call(
        functools.partial(kernel, n_strip, n_pt),
        out_shape=[whole, point],
        in_specs=[hbm] * 3,
        out_specs=[hbm, vmem],
        scratch_shapes=[
            pltpu.VMEM((total, 128), jnp.float32),
            pltpu.VMEM((total, 128), jnp.float32),
            pltpu.VMEM((8, 128), jnp.int32),
            pltpu.VMEM((8, 128), jnp.float32),
            pltpu.SMEM((NF,), jnp.float32),
            pltpu.SMEM((2, NF), jnp.float32),
            pltpu.VMEM((32, 128), jnp.float32),
            pltpu.VMEM((2, CH, 2, rows, 128), jnp.float32),
            pltpu.VMEM((2, CH, 2, rows, 128), jnp.float32),
            pltpu.VMEM((2, CH, 8, 128), jnp.float32),
            pltpu.VMEM((2, CH, 2, 8, 128), jnp.float32),
            sem((CH,)),
            sem((CH,)),
            sem((2,)),
            sem((2, CH, 4)),
            sem((2, CH, 4)),
        ],
        compiler_params=pltpu.CompilerParams(
            collective_id=0, has_side_effects=True, vmem_limit_bytes=60 * 1024 * 1024
        ),
        cost_estimate=pl.CostEstimate(
            flops=30 * total * 128, bytes_accessed=8 * total * 128, transcendentals=0
        ),
    )(courant, to_tiles(sea_mask[None]), to_tiles(spectra))
    result = pl.pallas_call(
        source_kernel,
        out_shape=whole,
        in_specs=[hbm] * 5,
        out_specs=hbm,
        scratch_shapes=[
            pltpu.VMEM((total, 128), jnp.float32),
            pltpu.VMEM((total, 128), jnp.float32),
            pltpu.VMEM((8, 128), jnp.float32),
            pltpu.VMEM((8, 128), jnp.float32),
            pltpu.VMEM((8, 128), jnp.int32),
            pltpu.VMEM((8, 128), jnp.float32),
            pltpu.VMEM((ND * 8, 128), jnp.float32),
            sem((CH,)),
            sem((CH,)),
            sem((4,)),
        ],
        compiler_params=pltpu.CompilerParams(vmem_limit_bytes=60 * 1024 * 1024),
        cost_estimate=pl.CostEstimate(
            flops=4 * total * 128, bytes_accessed=8 * total * 128, transcendentals=total * 128
        ),
    )(
        to_tiles(wind_speed[None]),
        to_tiles(wind_dir[None]),
        to_tiles(ice_mask[None]),
        mean_ratio,
        energy,
    )
    return from_tiles(result, spectra.shape)


def solution(mesh):
    in_specs = (
        P(None, "strip", "pt"),
        P(),
        P("strip", "pt"),
        P("strip", "pt"),
        P("strip", "pt"),
        P("strip", "pt"),
    )
    return jax.shard_map(
        functools.partial(on_device, mesh.shape["strip"], mesh.shape["pt"]),
        mesh=mesh,
        in_specs=in_specs,
        out_specs=P(None, "strip", "pt"),
        check_vma=False,
    )
```

```python
import functools
import numpy as np
import jax
import jax.numpy as jnp
from jax import lax
from jax.experimental import pallas as pl
from jax.experimental.pallas import tpu as pltpu
from jax.sharding import PartitionSpec as P

NF = 25
ND = 24
HALF = ND // 2
CH = 5
IC = NF // CH
RPI = ND * 8
RPC = RPI * IC
PAD = 8
MESH = pl.DeviceIdType.MESH

THETA = (np.float32(2.0 * np.pi) * np.arange(ND, dtype=np.float32) / np.float32(ND)).astype(np.float32)
COS = np.cos(THETA).astype(np.float32)
SIN = np.sin(THETA).astype(np.float32)
RATIO = np.float32(1.1) ** np.arange(NF, dtype=np.float32)
WEIGHT = (RATIO / (ND * np.sum(RATIO, dtype=np.float64))).astype(np.float32)
FROM_WEST = [d for d in range(ND) if COS[d] > 0.0]
FROM_EAST = [d for d in range(ND) if not COS[d] > 0.0]


def kernel(
    n_strip, n_pt,
    courant_in, sea_in, spectra,
    out, mean_ratio,
    e0, e1, sea_mask, courant, table,
    row_send, row_recv, col_send, col_recv,
    in_sem, out_sem, small_sem, send_sem, recv_sem,
):
    s = lax.axis_index("strip")
    p = lax.axis_index("pt")
    east = lax.rem(p + 1, n_pt)
    west = lax.rem(p + n_pt - 1, n_pt)
    has_south = s > 0
    has_north = s < n_strip - 1

    def load(c):
        rows = pl.ds(pl.multiple_of(c * RPC, RPC), RPC)
        held = pl.ds(pl.multiple_of(c * RPC + PAD, 8), RPC)
        return pltpu.make_async_copy(spectra.at[rows, :], e0.at[held, :], in_sem.at[c])

    def store(c):
        rows = pl.ds(pl.multiple_of(c * RPC, RPC), RPC)
        held = pl.ds(pl.multiple_of(c * RPC + PAD, 8), RPC)
        return pltpu.make_async_copy(e0.at[held, :], out.at[rows, :], out_sem.at[c])

    def rows_to(phase, c, way):
        return pltpu.make_async_remote_copy(
            src_ref=row_send.at[phase, c, way],
            dst_ref=row_recv.at[phase, c, way, pl.ds(PAD, IC * ND)],
            send_sem=send_sem.at[phase, c, way],
            recv_sem=recv_sem.at[phase, c, way],
            device_id={"strip": s + 1 if way == 0 else s - 1},
            device_id_type=MESH,
        )

    def cols_to(phase, c, way):
        return pltpu.make_async_remote_copy(
            src_ref=col_send.at[phase, c],
            dst_ref=col_recv.at[phase, c, way],
            send_sem=send_sem.at[phase, c, 2 + way],
            recv_sem=recv_sem.at[phase, c, 2 + way],
            device_id={"pt": east if way == 0 else west},
            device_id_type=MESH,
        )

    def send(phase, c):
        cols_to(phase, c, 0).start()
        cols_to(phase, c, 1).start()

        @pl.when(has_north)
        def _():
            rows_to(phase, c, 0).start()

        @pl.when(has_south)
        def _():
            rows_to(phase, c, 1).start()

    def receive(phase, c):
        cols_to(phase, c, 0).wait_recv()
        cols_to(phase, c, 1).wait_recv()

        @pl.when(has_south)
        def _():
            rows_to(phase, c, 0).wait_recv()

        @pl.when(has_north)
        def _():
            rows_to(phase, c, 1).wait_recv()

    smalls = [
        pltpu.make_async_copy(source, target, small_sem.at[n])
        for n, (source, target) in enumerate(
            ((courant_in, courant), (sea_in, sea_mask))
        )
    ]
    for c in range(CH):
        load(c).start()
    for small in smalls:
        small.start()

    barrier = pltpu.get_barrier_semaphore()
    for side in (east, west):
        pl.semaphore_signal(barrier, inc=1, device_id={"pt": side}, device_id_type=MESH)

    @pl.when(has_north)
    def _():
        pl.semaphore_signal(barrier, inc=1, device_id={"strip": s + 1}, device_id_type=MESH)

    @pl.when(has_south)
    def _():
        pl.semaphore_signal(barrier, inc=1, device_id={"strip": s - 1}, device_id_type=MESH)

    @pl.when(jnp.logical_not(has_south))
    def _():
        row_recv[:, :, 0] = jnp.zeros(row_recv.shape[:2] + row_recv.shape[3:], jnp.float32)

    @pl.when(jnp.logical_not(has_north))
    def _():
        row_recv[:, :, 1] = jnp.zeros(row_recv.shape[:2] + row_recv.shape[3:], jnp.float32)

    for i in range(NF):
        table[0, i] = float(WEIGHT[i])
        table[1, i] = float(WEIGHT[i] * RATIO[i])
    blank = jnp.zeros((PAD, 128), jnp.float32)
    for buffer in (e0, e1):
        buffer[pl.ds(0, PAD), :] = blank
        buffer[pl.ds(buffer.shape[0] - PAD, PAD), :] = blank
    lane = lax.broadcasted_iota(jnp.int32, (8, 128), 1)
    sub = lax.broadcasted_iota(jnp.int32, (8, 128), 0)
    low = sub < 4
    first_lane = lane == 0
    last_lane = lane == 127
    spot = jnp.where(low, lane - 1, lane)
    row = lax.rem(sub, 4)
    row_is = [row == j for j in range(4)]

    def base_of(c):
        return pl.multiple_of(c * RPC, 8) + PAD

    def pack_rows(src, phase, c):
        base = base_of(c)
        for il in range(IC):
            for way in range(2):
                for g in range(HALF // 4):
                    at = base + il * RPI + (HALF * way + 4 * g) * 8
                    edge = 3 - 3 * way
                    parts = [src[pl.ds(at + 8 * j + edge - j, 8), :] for j in range(4)]
                    packed = parts[0]
                    for j in range(1, 4):
                        packed = jnp.where(row_is[j], parts[j], packed)
                    row_send[phase, c, way, pl.ds(il * ND + 8 * g, 8), :] = packed

    def put(acc, n, pos, neg):
        mixed = jnp.where(low, neg, pos)
        return jnp.where(spot == n, pltpu.roll(mixed, n + 1, 1), acc)

    def pack_cols(src, phase, c):
        base = base_of(c)
        acc = jnp.zeros((8, 128), jnp.float32)
        for il in range(IC):
            for m in range(HALF):
                pos = src[pl.ds(base + il * RPI + 8 * FROM_WEST[m], 8), :]
                neg = src[pl.ds(base + il * RPI + 8 * FROM_EAST[m], 8), :]
                acc = put(acc, il * HALF + m, pos, neg)
        col_send[phase, c] = acc

    load(0).wait()
    pack_cols(e0, 0, 0)
    pack_rows(e0, 0, 0)
    pl.semaphore_wait(
        barrier, 2 + has_north.astype(jnp.int32) + has_south.astype(jnp.int32)
    )
    send(0, 0)

    def first_halo(c, carry):
        load(c).wait()
        pack_cols(e0, 0, c)
        pack_rows(e0, 0, c)
        send(0, c)
        return carry

    lax.fori_loop(1, CH, first_halo, 0)
    for small in smalls:
        small.wait()
    sea = sea_mask[...].astype(jnp.float32)

    def advance(src, dst, phase, c, sums):
        receive(phase, c)
        base = base_of(c)
        m0, m1 = sums
        halo = pltpu.roll(jnp.where(low, col_recv[phase, c, 1], col_recv[phase, c, 0]), 4, 0)
        acc = jnp.zeros((8, 128), jnp.float32)
        for il in range(IC):
            i = c * IC + il
            speed = courant[i] * sea
            keep = [sea - speed * float(k) for k in (np.abs(COS[:4]) + np.abs(SIN[:4]))]
            total = jnp.zeros((8, 128), jnp.float32)

            def step(d, core, side):
                at = base + il * RPI + 8 * d
                way, m = d // HALF, d % HALF
                edge = 3 * way
                near = src[pl.ds(at - 1 + 2 * way, 8), :]
                beyond = row_recv[
                    phase, c, way, pl.ds(PAD + il * ND + m // 4 * 8 + m % 4 - edge, 8), :
                ]
                near = jnp.where(row_is[edge], beyond, near)
                flow = float(abs(COS[d])) * side + float(abs(SIN[d])) * near
                q = d % 6
                fresh = keep[q if q < 4 else 6 - q] * core + speed * flow
                dst[pl.ds(at, 8), :] = fresh
                return fresh

            for m in range(HALF):
                n = il * HALF + m
                at_pos = base + il * RPI + 8 * FROM_WEST[m]
                at_neg = base + il * RPI + 8 * FROM_EAST[m]
                pos = src[pl.ds(at_pos, 8), :]
                neg = src[pl.ds(at_neg, 8), :]
                edge = pltpu.roll(halo, 127 - n, 1)
                seam_pos = jnp.where(low, edge, src[pl.ds(at_pos - 4, 8), :])
                seam_neg = jnp.where(low, src[pl.ds(at_neg + 4, 8), :], edge)
                side_pos = pltpu.roll(jnp.where(last_lane, seam_pos, pos), 1, 1)
                side_neg = pltpu.roll(jnp.where(first_lane, seam_neg, neg), 127, 1)
                new_pos = step(FROM_WEST[m], pos, side_pos)
                new_neg = step(FROM_EAST[m], neg, side_neg)
                if phase == 0:
                    acc = put(acc, n, new_pos, new_neg)
                else:
                    total = total + (new_pos + new_neg)
            if phase == 1:
                m0 = m0 + table[0, i] * total
                m1 = m1 + table[1, i] * total
        if phase == 0:
            col_send[1, c] = acc
        return m0, m1

    zero = jnp.zeros((8, 128), jnp.float32)

    def first_step(c, carry):
        advance(e0, e1, 0, c, (zero, zero))
        pack_rows(e1, 1, c)
        send(1, c)
        return carry

    lax.fori_loop(0, CH, first_step, 0)

    def second_step(c, sums):
        sums = advance(e1, e0, 1, c, sums)
        store(c).start()
        return sums

    m0, m1 = lax.fori_loop(0, CH, second_step, (zero, zero))
    mean_ratio[...] = m1 / jnp.maximum(m0, 0.05)

    def finish(c, carry):
        for phase in range(2):
            @pl.when(has_north)
            def _():
                rows_to(phase, c, 0).wait_send()

            @pl.when(has_south)
            def _():
                rows_to(phase, c, 1).wait_send()

            cols_to(phase, c, 0).wait_send()
            cols_to(phase, c, 1).wait_send()
        store(c).wait()
        return carry

    lax.fori_loop(0, CH, finish, 0)


def source_kernel(
    wind_speed_in, wind_dir_in, ice_in, mean_ratio_in, energy,
    out,
    held, done, wind_speed, wind_dir, ice_mask, mean_ratio, gain,
    in_sem, out_sem, small_sem,
):
    loads = [
        pltpu.make_async_copy(
            energy.at[pl.ds(c * RPC, RPC), :], held.at[pl.ds(c * RPC, RPC), :], in_sem.at[c]
        )
        for c in range(CH)
    ]
    stores = [
        pltpu.make_async_copy(
            done.at[pl.ds(c * RPC, RPC), :], out.at[pl.ds(c * RPC, RPC), :], out_sem.at[c]
        )
        for c in range(CH)
    ]
    smalls = [
        pltpu.make_async_copy(source, target, small_sem.at[n])
        for n, (source, target) in enumerate(
            (
                (wind_dir_in, wind_dir),
                (wind_speed_in, wind_speed),
                (ice_in, ice_mask),
                (mean_ratio_in, mean_ratio),
            )
        )
    ]
    for copy in smalls + loads:
        copy.start()
    for copy in smalls:
        copy.wait()
    ice = ice_mask[...].astype(jnp.float32)
    strength = (1.0 - ice) * 0.05 * wind_speed[...]
    cos_wind = strength * jnp.cos(wind_dir[...])
    sin_wind = strength * jnp.sin(wind_dir[...])
    for d in range(ND):
        gain[pl.ds(8 * d, 8), :] = jnp.maximum(
            float(COS[d]) * cos_wind + float(SIN[d]) * sin_wind, 0.0
        )
    drag = 0.02 * mean_ratio[...]
    cold = 0.7 * ice
    for c in range(CH):
        loads[c].wait()
        losses = [float(RATIO[c * IC + il]) * drag + cold for il in range(IC)]

        def one(d, carry):
            push = gain[pl.ds(pl.multiple_of(8 * d, 8), 8), :]
            for il in range(IC):
                rows = pl.ds(pl.multiple_of((c * IC + il) * RPI + 8 * d, 8), 8)
                net = float(RATIO[c * IC + il]) * push - losses[il]
                done[rows, :] = held[rows, :] * jnp.exp(net)
            return carry

        lax.fori_loop(0, ND, one, 0, unroll=8)
        stores[c].start()
    for copy in stores:
        copy.wait()


def to_tiles(x):
    lead, rows, cols = x.shape
    x = x.reshape(lead, rows, cols // 128, 128).transpose(0, 2, 1, 3)
    return x.reshape(lead * rows * cols // 128, 128)


def from_tiles(x, shape):
    lead, rows, cols = shape
    x = x.reshape(lead, cols // 128, rows, 128).transpose(0, 2, 1, 3)
    return x.reshape(shape)


def on_device(n_strip, n_pt, spectra, courant, wind_speed, wind_dir, sea_mask, ice_mask):
    total = spectra.shape[0] * 8
    vmem = pl.BlockSpec(memory_space=pltpu.VMEM)
    hbm = pl.BlockSpec(memory_space=pl.ANY)
    sem = pltpu.SemaphoreType.DMA
    rows = IC * ND
    whole = jax.ShapeDtypeStruct((total, 128), jnp.float32)
    point = jax.ShapeDtypeStruct((8, 128), jnp.float32)
    energy, mean_ratio = pl.pallas_call(
        functools.partial(kernel, n_strip, n_pt),
        out_shape=[whole, point],
        in_specs=[hbm] * 3,
        out_specs=[hbm, vmem],
        scratch_shapes=[
            pltpu.VMEM((total + 2 * PAD, 128), jnp.float32),
            pltpu.VMEM((total + 2 * PAD, 128), jnp.float32),
            pltpu.VMEM((8, 128), jnp.int32),
            pltpu.SMEM((NF,), jnp.float32),
            pltpu.SMEM((2, NF), jnp.float32),
            pltpu.VMEM((2, CH, 2, rows, 128), jnp.float32),
            pltpu.VMEM((2, CH, 2, rows + 2 * PAD, 128), jnp.float32),
            pltpu.VMEM((2, CH, 8, 128), jnp.float32),
            pltpu.VMEM((2, CH, 2, 8, 128), jnp.float32),
            sem((CH,)),
            sem((CH,)),
            sem((2,)),
            sem((2, CH, 4)),
            sem((2, CH, 4)),
        ],
        compiler_params=pltpu.CompilerParams(
            collective_id=0, has_side_effects=True, vmem_limit_bytes=60 * 1024 * 1024
        ),
        cost_estimate=pl.CostEstimate(
            flops=30 * total * 128, bytes_accessed=8 * total * 128, transcendentals=0
        ),
    )(courant, to_tiles(sea_mask[None]), to_tiles(spectra))
    result = pl.pallas_call(
        source_kernel,
        out_shape=whole,
        in_specs=[hbm] * 5,
        out_specs=hbm,
        scratch_shapes=[
            pltpu.VMEM((total, 128), jnp.float32),
            pltpu.VMEM((total, 128), jnp.float32),
            pltpu.VMEM((8, 128), jnp.float32),
            pltpu.VMEM((8, 128), jnp.float32),
            pltpu.VMEM((8, 128), jnp.int32),
            pltpu.VMEM((8, 128), jnp.float32),
            pltpu.VMEM((ND * 8, 128), jnp.float32),
            sem((CH,)),
            sem((CH,)),
            sem((4,)),
        ],
        compiler_params=pltpu.CompilerParams(vmem_limit_bytes=60 * 1024 * 1024),
        cost_estimate=pl.CostEstimate(
            flops=4 * total * 128, bytes_accessed=8 * total * 128, transcendentals=total * 128
        ),
    )(
        to_tiles(wind_speed[None]),
        to_tiles(wind_dir[None]),
        to_tiles(ice_mask[None]),
        mean_ratio,
        energy,
    )
    return from_tiles(result, spectra.shape)


def solution(mesh):
    in_specs = (
        P(None, "strip", "pt"),
        P(),
        P("strip", "pt"),
        P("strip", "pt"),
        P("strip", "pt"),
        P("strip", "pt"),
    )
    return jax.shard_map(
        functools.partial(on_device, mesh.shape["strip"], mesh.shape["pt"]),
        mesh=mesh,
        in_specs=in_specs,
        out_specs=P(None, "strip", "pt"),
        check_vma=False,
    )
```

```python
import functools
import numpy as np
import jax
import jax.numpy as jnp
from jax import lax
from jax.experimental import pallas as pl
from jax.experimental.pallas import tpu as pltpu
from jax.sharding import PartitionSpec as P

NF = 25
ND = 24
HALF = ND // 2
CH = 5
IC = NF // CH
RPI = ND * 8
RPC = RPI * IC
GROUPS = NF // 8
LAST = NF - 1
QUAD = ND // 4
MESH = pl.DeviceIdType.MESH

THETA = (np.float32(2.0 * np.pi) * np.arange(ND, dtype=np.float32) / np.float32(ND)).astype(np.float32)
COS = np.cos(THETA).astype(np.float32)
SIN = np.sin(THETA).astype(np.float32)
RATIO = np.float32(1.1) ** np.arange(NF, dtype=np.float32)
WEIGHT = (RATIO / (ND * np.sum(RATIO, dtype=np.float64))).astype(np.float32)
PAIRS = [(m, QUAD + m, 0) for m in range(QUAD)]
PAIRS += [(3 * QUAD + m, 2 * QUAD + m, 1) for m in range(QUAD)]
LAST_PAIRS = [(0, 1, 0), (3, 2, 1)]


def kernel(
    n_strip, n_pt,
    courant_in, sea_in, spectra,
    out, mean_ratio,
    e0, e1, e2, l0, l1, l2,
    sea_mask, sea, courant, speed, weight, sums,
    halo, last_halo, col_send, col_recv,
    in_sem, out_sem, small_sem, row_send_sem, row_recv_sem, col_send_sem, col_recv_sem,
):
    s = lax.axis_index("strip")
    p = lax.axis_index("pt")
    east = lax.rem(p + 1, n_pt)
    west = lax.rem(p + n_pt - 1, n_pt)
    has_south = s > 0
    has_north = s < n_strip - 1

    def load(i):
        return pltpu.make_async_copy(
            spectra.at[i], e0.at[i // 8, :, :, i % 8, :], in_sem.at[i]
        )

    def load_last(d):
        return pltpu.make_async_copy(
            spectra.at[LAST, d], l0.at[d // QUAD, :, d % QUAD, :], in_sem.at[LAST + d]
        )

    def store(g, j):
        return pltpu.make_async_copy(
            e2.at[g, :, :, j, :], out.at[g * 8 + j], out_sem.at[g * 8 + j]
        )

    def store_last(d):
        return pltpu.make_async_copy(
            l2.at[d // QUAD, :, d % QUAD, :], out.at[LAST, d], out_sem.at[LAST + d]
        )

    def rows_to(phase, c, way, tile):
        edge = 4 * tile + 3 - 3 * way
        if isinstance(c, int) and c == GROUPS:
            held = (l0, l1)[phase]
            source = held.at[pl.ds(2 * way, 2), edge]
            target = last_halo.at[phase, way, tile]
        else:
            held = (e0, e1)[phase]
            source = held.at[c, pl.ds(HALF * way, HALF), edge]
            target = halo.at[phase, c, way, tile]
        return pltpu.make_async_remote_copy(
            src_ref=source,
            dst_ref=target,
            send_sem=row_send_sem.at[phase, c, way, tile],
            recv_sem=row_recv_sem.at[phase, c, way, tile],
            device_id={"strip": s + 1 if way == 0 else s - 1},
            device_id_type=MESH,
        )

    def cols_to(phase, c, way):
        return pltpu.make_async_remote_copy(
            src_ref=col_send.at[phase, c],
            dst_ref=col_recv.at[phase, c, way],
            send_sem=col_send_sem.at[phase, c, way],
            recv_sem=col_recv_sem.at[phase, c, way],
            device_id={"pt": east if way == 0 else west},
            device_id_type=MESH,
        )

    def send_rows(phase, c):
        @pl.when(has_north)
        def _():
            rows_to(phase, c, 0, 0).start()
            rows_to(phase, c, 0, 1).start()

        @pl.when(has_south)
        def _():
            rows_to(phase, c, 1, 0).start()
            rows_to(phase, c, 1, 1).start()

    def send_cols(phase, c):
        cols_to(phase, c, 0).start()
        cols_to(phase, c, 1).start()

    def receive(phase, c):
        cols_to(phase, c, 0).wait_recv()
        cols_to(phase, c, 1).wait_recv()

        @pl.when(has_south)
        def _():
            rows_to(phase, c, 0, 0).wait_recv()
            rows_to(phase, c, 0, 1).wait_recv()

        @pl.when(has_north)
        def _():
            rows_to(phase, c, 1, 0).wait_recv()
            rows_to(phase, c, 1, 1).wait_recv()

    smalls = [
        pltpu.make_async_copy(source, target, small_sem.at[n])
        for n, (source, target) in enumerate(((courant_in, courant), (sea_in, sea_mask)))
    ]
    for i in range(LAST):
        load(i).start()
    for small in smalls:
        small.start()

    barrier = pltpu.get_barrier_semaphore()
    for side in (east, west):
        pl.semaphore_signal(barrier, inc=1, device_id={"pt": side}, device_id_type=MESH)

    @pl.when(has_north)
    def _():
        pl.semaphore_signal(barrier, inc=1, device_id={"strip": s + 1}, device_id_type=MESH)

    @pl.when(has_south)
    def _():
        pl.semaphore_signal(barrier, inc=1, device_id={"strip": s - 1}, device_id_type=MESH)

    zero = jnp.zeros((8, 128), jnp.float32)
    l0[...] = jnp.zeros(l0.shape, jnp.float32)
    for d in range(ND):
        load_last(d).start()

    @pl.when(jnp.logical_not(has_south))
    def _():
        halo[:, :, 0] = jnp.zeros(halo.shape[:2] + halo.shape[3:], jnp.float32)
        last_halo[:, 0] = jnp.zeros(last_halo.shape[:1] + last_halo.shape[2:], jnp.float32)

    @pl.when(jnp.logical_not(has_north))
    def _():
        halo[:, :, 1] = jnp.zeros(halo.shape[:2] + halo.shape[3:], jnp.float32)
        last_halo[:, 1] = jnp.zeros(last_halo.shape[:1] + last_halo.shape[2:], jnp.float32)

    lane = lax.broadcasted_iota(jnp.int32, (8, 128), 1)
    sub = lax.broadcasted_iota(jnp.int32, (8, 128), 0)
    couple = lane // 2
    even = lax.rem(lane, 2) == 0
    first_lane = lane == 0
    last_lane = lane == 127

    def by_sub(values):
        made = zero
        for j, value in enumerate(values):
            made = jnp.where(sub == j, value, made)
        return made

    for small in smalls:
        small.wait()
    for g in range(GROUPS):
        speed[g] = by_sub([courant[8 * g + j] for j in range(8)])
        weight[0, g] = by_sub([float(WEIGHT[8 * g + j]) for j in range(8)])
        weight[1, g] = by_sub([float(WEIGHT[8 * g + j] * RATIO[8 * g + j]) for j in range(8)])
    sea_now = sea_mask[...].astype(jnp.float32)
    for t in range(8):
        sea[t] = jnp.broadcast_to(sea_now[t : t + 1], (8, 128))

    def put(acc, n, pos, neg):
        mixed = pltpu.roll(jnp.where(last_lane, pos, neg), 2 * n + 1, 1)
        return jnp.where(couple == n, mixed, acc)

    def pack_cols(src, pairs):
        acc = zero
        for n, (west_block, east_block, _) in enumerate(pairs):
            for y in range(4):
                acc = put(acc, 4 * n + y, src[west_block, 4 + y], src[east_block, y])
        return acc

    def first_halo(c, carry):
        send_rows(0, c)
        col_send[0, c] = pack_cols(e0.at[c], PAIRS)
        send_cols(0, c)
        return carry

    for j in range(8):
        load(j).wait()
    pl.semaphore_wait(
        barrier, 2 + has_north.astype(jnp.int32) + has_south.astype(jnp.int32)
    )

    def loaded(c, carry):
        @pl.when(c > 0)
        def _():
            for j in range(8):
                pltpu.make_async_copy(
                    spectra.at[c * 8 + j], e0.at[c, :, :, j, :], in_sem.at[c * 8 + j]
                ).wait()

        return first_halo(c, carry)

    lax.fori_loop(0, GROUPS, loaded, 0)
    for d in range(ND):
        load_last(d).wait()
    send_rows(0, GROUPS)
    col_send[0, GROUPS] = pack_cols(l0, LAST_PAIRS)
    send_cols(0, GROUPS)

    def advance(phase, c, src, dst, row_halo, pairs, coefficients):
        edges = jnp.where(even, pltpu.roll(col_recv[phase, c, 0], 2, 1), col_recv[phase, c, 1])
        acc = zero
        totals = [zero] * 8
        for n, (west_block, east_block, way) in enumerate(pairs):
            near_halo = [
                [row_halo[way, t, block - way * (len(pairs))] for t in range(2)]
                for block in (west_block, east_block)
            ]
            cores = [
                [[src[block, 4 * t + y] for t in range(2)] for y in range(4)]
                for block in (west_block, east_block)
            ]
            terms = [coefficients(block) for block in (west_block, east_block)]
            for y in range(4):
                edge = pltpu.roll(edges, 128 - (2 * (4 * n + y) + 2), 1)
                w0, w1 = [pltpu.roll(x, 1, 1) for x in cores[0][y]]
                x0, x1 = [pltpu.roll(x, 127, 1) for x in cores[1][y]]
                sides = (
                    (jnp.where(first_lane, edge, w0), jnp.where(first_lane, w0, w1)),
                    (jnp.where(last_lane, x1, x0), jnp.where(last_lane, edge, x1)),
                )
                back = y - 1 + 2 * way
                fresh = []
                for k, block in enumerate((west_block, east_block)):
                    along, across, keep = terms[k]
                    near = cores[k][back] if 0 <= back < 4 else near_halo[k]
                    for t in range(2):
                        moved = keep * cores[k][y][t] + (along * sides[k][t] + across * near[t])
                        moved = moved * sea[4 * t + y]
                        dst[block, 4 * t + y] = moved
                        fresh.append(moved)
                if phase == 0:
                    acc = put(acc, 4 * n + y, fresh[1], fresh[2])
                else:
                    totals[y] = totals[y] + (fresh[0] + fresh[2])
                    totals[4 + y] = totals[4 + y] + (fresh[1] + fresh[3])
        if phase == 0:
            col_send[1, c] = acc
        return totals

    def group(phase, c):
        now = speed[c]

        def coefficients(d):
            cos, sin = float(abs(COS[d])), float(abs(SIN[d]))
            return cos * now, sin * now, 1.0 - (cos + sin) * now

        src, dst = ((e0, e1), (e1, e2))[phase]
        receive(phase, c)
        return advance(
            phase, c, src.at[c], dst.at[c], halo.at[phase, c], PAIRS, coefficients
        )

    def leftover(phase):
        now = courant[LAST]

        def coefficients(q):
            cos = by_sub([float(abs(COS[QUAD * q + j])) for j in range(QUAD)])
            sin = by_sub([float(abs(SIN[QUAD * q + j])) for j in range(QUAD)])
            return cos * now, sin * now, 1.0 - (cos + sin) * now

        src, dst = ((l0, l1), (l1, l2))[phase]
        receive(phase, GROUPS)
        return advance(
            phase, GROUPS, src, dst, last_halo.at[phase], LAST_PAIRS, coefficients
        )

    def first_step(c, carry):
        group(0, c)
        send_cols(1, c)
        send_rows(1, c)
        return carry

    lax.fori_loop(0, GROUPS, first_step, 0)
    leftover(0)
    send_cols(1, GROUPS)
    send_rows(1, GROUPS)

    sums[...] = jnp.zeros(sums.shape, jnp.float32)

    def second_step(c, carry):
        totals = group(1, c)
        for j in range(8):
            store(c, j).start()
        for t in range(8):
            sums[0, t] = sums[0, t] + weight[0, c] * totals[t]
            sums[1, t] = sums[1, t] + weight[1, c] * totals[t]
        return carry

    lax.fori_loop(0, GROUPS, second_step, 0)
    totals = leftover(1)
    for d in range(ND):
        store_last(d).start()
    for t in range(8):
        rest = jnp.where(sub < QUAD, totals[t], 0.0)
        m0 = sums[0, t] + float(WEIGHT[LAST]) * rest
        m1 = sums[1, t] + float(WEIGHT[LAST] * RATIO[LAST]) * rest
        m0 = jnp.sum(m0, axis=0, keepdims=True)
        m1 = jnp.sum(m1, axis=0, keepdims=True)
        mean_ratio[pl.ds(t, 1), :] = m1 / jnp.maximum(m0, 0.05)

    for phase in range(2):
        for c in range(GROUPS + 1):
            @pl.when(has_north)
            def _():
                rows_to(phase, c, 0, 0).wait_send()
                rows_to(phase, c, 0, 1).wait_send()

            @pl.when(has_south)
            def _():
                rows_to(phase, c, 1, 0).wait_send()
                rows_to(phase, c, 1, 1).wait_send()

            cols_to(phase, c, 0).wait_send()
            cols_to(phase, c, 1).wait_send()
    for i in range(LAST):
        store(i // 8, i % 8).wait()
    for d in range(ND):
        store_last(d).wait()


def source_kernel(
    wind_speed_in, wind_dir_in, ice_in, mean_ratio_in, energy,
    out,
    held, done, wind_speed, wind_dir, ice_mask, mean_ratio, gain,
    in_sem, out_sem, small_sem,
):
    loads = [
        pltpu.make_async_copy(
            energy.at[pl.ds(c * RPC, RPC), :], held.at[pl.ds(c * RPC, RPC), :], in_sem.at[c]
        )
        for c in range(CH)
    ]
    stores = [
        pltpu.make_async_copy(
            done.at[pl.ds(c * RPC, RPC), :], out.at[pl.ds(c * RPC, RPC), :], out_sem.at[c]
        )
        for c in range(CH)
    ]
    smalls = [
        pltpu.make_async_copy(source, target, small_sem.at[n])
        for n, (source, target) in enumerate(
            (
                (wind_dir_in, wind_dir),
                (wind_speed_in, wind_speed),
                (ice_in, ice_mask),
                (mean_ratio_in, mean_ratio),
            )
        )
    ]
    for copy in smalls + loads:
        copy.start()
    for copy in smalls:
        copy.wait()
    ice = ice_mask[...].astype(jnp.float32)
    strength = (1.0 - ice) * 0.05 * wind_speed[...]
    cos_wind = strength * jnp.cos(wind_dir[...])
    sin_wind = strength * jnp.sin(wind_dir[...])
    for d in range(ND):
        gain[pl.ds(8 * d, 8), :] = jnp.maximum(
            float(COS[d]) * cos_wind + float(SIN[d]) * sin_wind, 0.0
        )
    drag = 0.02 * mean_ratio[...]
    cold = 0.7 * ice
    for c in range(CH):
        loads[c].wait()
        losses = [float(RATIO[c * IC + il]) * drag + cold for il in range(IC)]

        def one(d, carry):
            push = gain[pl.ds(pl.multiple_of(8 * d, 8), 8), :]
            for il in range(IC):
                rows = pl.ds(pl.multiple_of((c * IC + il) * RPI + 8 * d, 8), 8)
                net = float(RATIO[c * IC + il]) * push - losses[il]
                done[rows, :] = held[rows, :] * jnp.exp(net)
            return carry

        lax.fori_loop(0, ND, one, 0, unroll=8)
        stores[c].start()
    for copy in stores:
        copy.wait()


def to_tiles(x):
    lead, rows, cols = x.shape
    x = x.reshape(lead, rows, cols // 128, 128).transpose(0, 2, 1, 3)
    return x.reshape(lead * rows * cols // 128, 128)


def from_tiles(x, shape):
    lead, rows, cols = shape
    x = x.reshape(lead, cols // 128, rows, 128).transpose(0, 2, 1, 3)
    return x.reshape(shape)


def on_device(n_strip, n_pt, spectra, courant, wind_speed, wind_dir, sea_mask, ice_mask):
    total = spectra.shape[0] * 8
    vmem = pl.BlockSpec(memory_space=pltpu.VMEM)
    hbm = pl.BlockSpec(memory_space=pl.ANY)
    sem = pltpu.SemaphoreType.DMA
    whole = jax.ShapeDtypeStruct((total, 128), jnp.float32)
    tiles = (NF, ND, 8, 128)
    blocks = pltpu.VMEM((GROUPS, ND, 8, 8, 128), jnp.float32)
    last_blocks = pltpu.VMEM((4, 8, 8, 128), jnp.float32)
    energy, mean_ratio = pl.pallas_call(
        functools.partial(kernel, n_strip, n_pt),
        out_shape=[
            jax.ShapeDtypeStruct(tiles, jnp.float32),
            jax.ShapeDtypeStruct((8, 128), jnp.float32),
        ],
        in_specs=[hbm] * 3,
        out_specs=[hbm, vmem],
        scratch_shapes=[
            blocks,
            blocks,
            blocks,
            last_blocks,
            last_blocks,
            last_blocks,
            pltpu.VMEM((8, 128), jnp.int32),
            pltpu.VMEM((8, 8, 128), jnp.float32),
            pltpu.SMEM((NF,), jnp.float32),
            pltpu.VMEM((GROUPS, 8, 128), jnp.float32),
            pltpu.VMEM((2, GROUPS, 8, 128), jnp.float32),
            pltpu.VMEM((2, 8, 8, 128), jnp.float32),
            pltpu.VMEM((2, GROUPS, 2, 2, HALF, 8, 128), jnp.float32),
            pltpu.VMEM((2, 2, 2, 2, 8, 128), jnp.float32),
            pltpu.VMEM((2, GROUPS + 1, 8, 128), jnp.float32),
            pltpu.VMEM((2, GROUPS + 1, 2, 8, 128), jnp.float32),
            sem((LAST + ND,)),
            sem((LAST + ND,)),
            sem((2,)),
            sem((2, GROUPS + 1, 2, 2)),
            sem((2, GROUPS + 1, 2, 2)),
            sem((2, GROUPS + 1, 2)),
            sem((2, GROUPS + 1, 2)),
        ],
        compiler_params=pltpu.CompilerParams(
            collective_id=0, has_side_effects=True, vmem_limit_bytes=60 * 1024 * 1024
        ),
        cost_estimate=pl.CostEstimate(
            flops=16 * total * 128, bytes_accessed=8 * total * 128, transcendentals=0
        ),
    )(courant, to_tiles(sea_mask[None]), to_tiles(spectra).reshape(tiles))
    result = pl.pallas_call(
        source_kernel,
        out_shape=whole,
        in_specs=[hbm] * 5,
        out_specs=hbm,
        scratch_shapes=[
            pltpu.VMEM((total, 128), jnp.float32),
            pltpu.VMEM((total, 128), jnp.float32),
            pltpu.VMEM((8, 128), jnp.float32),
            pltpu.VMEM((8, 128), jnp.float32),
            pltpu.VMEM((8, 128), jnp.int32),
            pltpu.VMEM((8, 128), jnp.float32),
            pltpu.VMEM((ND * 8, 128), jnp.float32),
            sem((CH,)),
            sem((CH,)),
            sem((4,)),
        ],
        compiler_params=pltpu.CompilerParams(vmem_limit_bytes=60 * 1024 * 1024),
        cost_estimate=pl.CostEstimate(
            flops=4 * total * 128, bytes_accessed=8 * total * 128, transcendentals=total * 128
        ),
    )(
        to_tiles(wind_speed[None]),
        to_tiles(wind_dir[None]),
        to_tiles(ice_mask[None]),
        mean_ratio,
        energy.reshape(total, 128),
    )
    return from_tiles(result, spectra.shape)


def solution(mesh):
    in_specs = (
        P(None, "strip", "pt"),
        P(),
        P("strip", "pt"),
        P("strip", "pt"),
        P("strip", "pt"),
        P("strip", "pt"),
    )
    return jax.shard_map(
        functools.partial(on_device, mesh.shape["strip"], mesh.shape["pt"]),
        mesh=mesh,
        in_specs=in_specs,
        out_specs=P(None, "strip", "pt"),
        check_vma=False,
    )
```

```python
import functools
import numpy as np
import jax
import jax.numpy as jnp
from jax import lax
from jax.experimental import pallas as pl
from jax.experimental.pallas import tpu as pltpu
from jax.sharding import PartitionSpec as P

NF = 25
ND = 24
HALF = ND // 2
CH = 5
IC = NF // CH
RPI = ND * 8
RPC = RPI * IC
RPG = RPI * 8
GROUPS = NF // 8
LAST = NF - 1
QUAD = ND // 4
MESH = pl.DeviceIdType.MESH

THETA = (np.float32(2.0 * np.pi) * np.arange(ND, dtype=np.float32) / np.float32(ND)).astype(np.float32)
COS = np.cos(THETA).astype(np.float32)
SIN = np.sin(THETA).astype(np.float32)
RATIO = np.float32(1.1) ** np.arange(NF, dtype=np.float32)
WEIGHT = (RATIO / (ND * np.sum(RATIO, dtype=np.float64))).astype(np.float32)
PAIRS = [(m, QUAD + m, 0) for m in range(QUAD)]
PAIRS += [(3 * QUAD + m, 2 * QUAD + m, 1) for m in range(QUAD)]
LAST_PAIRS = [(0, 1, 0), (3, 2, 1)]


def kernel(
    n_strip, n_pt,
    courant_in, sea_in, spectra,
    out, mean_ratio,
    raw, done, e0, e1, l0, l1,
    sea_mask, sea, courant, speed, weight, sums,
    halo, last_halo, col_send, col_recv,
    in_sem, out_sem, small_sem, row_send_sem, row_recv_sem, col_send_sem, col_recv_sem,
):
    s = lax.axis_index("strip")
    p = lax.axis_index("pt")
    east = lax.rem(p + 1, n_pt)
    west = lax.rem(p + n_pt - 1, n_pt)
    has_south = s > 0
    has_north = s < n_strip - 1

    def load(c):
        rows = pl.ds(c * RPG, RPI if isinstance(c, int) and c == GROUPS else RPG)
        return pltpu.make_async_copy(spectra.at[rows, :], raw.at[rows, :], in_sem.at[c])

    def store(c):
        rows = pl.ds(c * RPG, RPI if isinstance(c, int) and c == GROUPS else RPG)
        return pltpu.make_async_copy(done.at[rows, :], out.at[rows, :], out_sem.at[c])

    def rows_to(phase, c, way, tile):
        edge = 4 * tile + 3 - 3 * way
        if isinstance(c, int) and c == GROUPS:
            held = (l0, l1)[phase]
            source = held.at[pl.ds(2 * way, 2), edge]
            target = last_halo.at[phase, way, tile]
        else:
            held = (e0, e1)[phase]
            source = held.at[c, pl.ds(HALF * way, HALF), edge]
            target = halo.at[phase, c, way, tile]
        return pltpu.make_async_remote_copy(
            src_ref=source,
            dst_ref=target,
            send_sem=row_send_sem.at[phase, c, way, tile],
            recv_sem=row_recv_sem.at[phase, c, way, tile],
            device_id={"strip": s + 1 if way == 0 else s - 1},
            device_id_type=MESH,
        )

    def cols_to(phase, c, way):
        return pltpu.make_async_remote_copy(
            src_ref=col_send.at[phase, c],
            dst_ref=col_recv.at[phase, c, way],
            send_sem=col_send_sem.at[phase, c, way],
            recv_sem=col_recv_sem.at[phase, c, way],
            device_id={"pt": east if way == 0 else west},
            device_id_type=MESH,
        )

    def send_rows(phase, c):
        @pl.when(has_north)
        def _():
            rows_to(phase, c, 0, 0).start()
            rows_to(phase, c, 0, 1).start()

        @pl.when(has_south)
        def _():
            rows_to(phase, c, 1, 0).start()
            rows_to(phase, c, 1, 1).start()

    def send_cols(phase, c):
        cols_to(phase, c, 0).start()
        cols_to(phase, c, 1).start()

    def receive(phase, c):
        cols_to(phase, c, 0).wait_recv()
        cols_to(phase, c, 1).wait_recv()

        @pl.when(has_south)
        def _():
            rows_to(phase, c, 0, 0).wait_recv()
            rows_to(phase, c, 0, 1).wait_recv()

        @pl.when(has_north)
        def _():
            rows_to(phase, c, 1, 0).wait_recv()
            rows_to(phase, c, 1, 1).wait_recv()

    smalls = [
        pltpu.make_async_copy(source, target, small_sem.at[n])
        for n, (source, target) in enumerate(((courant_in, courant), (sea_in, sea_mask)))
    ]
    for c in range(GROUPS + 1):
        load(c).start()
    for small in smalls:
        small.start()

    barrier = pltpu.get_barrier_semaphore()
    for side in (east, west):
        pl.semaphore_signal(barrier, inc=1, device_id={"pt": side}, device_id_type=MESH)

    @pl.when(has_north)
    def _():
        pl.semaphore_signal(barrier, inc=1, device_id={"strip": s + 1}, device_id_type=MESH)

    @pl.when(has_south)
    def _():
        pl.semaphore_signal(barrier, inc=1, device_id={"strip": s - 1}, device_id_type=MESH)

    zero = jnp.zeros((8, 128), jnp.float32)
    raw[pl.ds(NF * RPI, 16), :] = jnp.zeros((16, 128), jnp.float32)

    @pl.when(jnp.logical_not(has_south))
    def _():
        halo[:, :, 0] = jnp.zeros(halo.shape[:2] + halo.shape[3:], jnp.float32)
        last_halo[:, 0] = jnp.zeros(last_halo.shape[:1] + last_halo.shape[2:], jnp.float32)

    @pl.when(jnp.logical_not(has_north))
    def _():
        halo[:, :, 1] = jnp.zeros(halo.shape[:2] + halo.shape[3:], jnp.float32)
        last_halo[:, 1] = jnp.zeros(last_halo.shape[:1] + last_halo.shape[2:], jnp.float32)

    lane = lax.broadcasted_iota(jnp.int32, (8, 128), 1)
    sub = lax.broadcasted_iota(jnp.int32, (8, 128), 0)
    couple = lane // 2
    even = lax.rem(lane, 2) == 0
    first_lane = lane == 0
    last_lane = lane == 127

    def by_sub(values):
        made = zero
        for j, value in enumerate(values):
            made = jnp.where(sub == j, value, made)
        return made

    for small in smalls:
        small.wait()
    for g in range(GROUPS):
        speed[g] = by_sub([courant[8 * g + j] for j in range(8)])
        weight[0, g] = by_sub([float(WEIGHT[8 * g + j]) for j in range(8)])
        weight[1, g] = by_sub([float(WEIGHT[8 * g + j] * RATIO[8 * g + j]) for j in range(8)])
    sea_now = sea_mask[...].astype(jnp.float32)
    for t in range(8):
        sea[t] = jnp.broadcast_to(sea_now[t : t + 1], (8, 128))

    def put(acc, n, pos, neg):
        mixed = pltpu.roll(jnp.where(last_lane, pos, neg), 2 * n + 1, 1)
        return jnp.where(couple == n, mixed, acc)

    def pack_cols(src, pairs):
        acc = zero
        for n, (west_block, east_block, _) in enumerate(pairs):
            for y in range(4):
                acc = put(acc, 4 * n + y, src[west_block, 4 + y], src[east_block, y])
        return acc

    pl.semaphore_wait(
        barrier, 2 + has_north.astype(jnp.int32) + has_south.astype(jnp.int32)
    )

    def gather(c, d, t):
        start = pl.multiple_of(c * RPG, 8) + d * 8 + t
        e0[c, d, t] = raw[pl.ds(start, 8, stride=RPI), :]

    def first_halo(c, carry):
        pltpu.make_async_copy(
            spectra.at[pl.ds(c * RPG, RPG), :], raw.at[pl.ds(c * RPG, RPG), :], in_sem.at[c]
        ).wait()
        outer = [(d, t) for d in range(ND) for t in ((3, 7) if d < HALF else (0, 4))]
        for d, t in outer:
            gather(c, d, t)
        send_rows(0, c)
        for d in range(ND):
            for t in range(8):
                if (d, t) not in outer:
                    gather(c, d, t)
        col_send[0, c] = pack_cols(e0.at[c], PAIRS)
        send_cols(0, c)
        return carry

    lax.fori_loop(0, GROUPS, first_halo, 0)
    load(GROUPS).wait()
    for q in range(4):
        for t in range(8):
            l0[q, t] = raw[pl.ds(LAST * RPI + q * QUAD * 8 + t, 8, stride=8), :]
    send_rows(0, GROUPS)
    col_send[0, GROUPS] = pack_cols(l0, LAST_PAIRS)
    send_cols(0, GROUPS)

    def advance(phase, c, src, write, row_halo, pairs, coefficients):
        edges = jnp.where(even, pltpu.roll(col_recv[phase, c, 0], 2, 1), col_recv[phase, c, 1])
        acc = zero
        totals = [zero] * 8
        for n, (west_block, east_block, way) in enumerate(pairs):
            near_halo = [
                [row_halo[way, t, block - way * (len(pairs))] for t in range(2)]
                for block in (west_block, east_block)
            ]
            cores = [
                [[src[block, 4 * t + y] for t in range(2)] for y in range(4)]
                for block in (west_block, east_block)
            ]
            terms = [coefficients(block) for block in (west_block, east_block)]
            for y in range(4):
                edge = pltpu.roll(edges, 128 - (2 * (4 * n + y) + 2), 1)
                w0, w1 = [pltpu.roll(x, 1, 1) for x in cores[0][y]]
                x0, x1 = [pltpu.roll(x, 127, 1) for x in cores[1][y]]
                sides = (
                    (jnp.where(first_lane, edge, w0), jnp.where(first_lane, w0, w1)),
                    (jnp.where(last_lane, x1, x0), jnp.where(last_lane, edge, x1)),
                )
                back = y - 1 + 2 * way
                fresh = []
                for k, block in enumerate((west_block, east_block)):
                    along, across, keep = terms[k]
                    near = cores[k][back] if 0 <= back < 4 else near_halo[k]
                    for t in range(2):
                        moved = keep * cores[k][y][t] + (along * sides[k][t] + across * near[t])
                        moved = moved * sea[4 * t + y]
                        write(block, 4 * t + y, moved)
                        fresh.append(moved)
                if phase == 0:
                    acc = put(acc, 4 * n + y, fresh[1], fresh[2])
                else:
                    totals[y] = totals[y] + (fresh[0] + fresh[2])
                    totals[4 + y] = totals[4 + y] + (fresh[1] + fresh[3])
        if phase == 0:
            col_send[1, c] = acc
        return totals

    def group(phase, c):
        now = speed[c]

        def coefficients(d):
            cos, sin = float(abs(COS[d])), float(abs(SIN[d]))
            return cos * now, sin * now, 1.0 - (cos + sin) * now

        def write(d, t, value):
            if phase == 0:
                e1[c, d, t] = value
            else:
                start = pl.multiple_of(c * RPG, 8) + d * 8 + t
                done[pl.ds(start, 8, stride=RPI), :] = value

        src = (e0, e1)[phase]
        receive(phase, c)
        return advance(
            phase, c, src.at[c], write, halo.at[phase, c], PAIRS, coefficients
        )

    def leftover(phase):
        now = courant[LAST]

        def coefficients(q):
            cos = by_sub([float(abs(COS[QUAD * q + j])) for j in range(QUAD)])
            sin = by_sub([float(abs(SIN[QUAD * q + j])) for j in range(QUAD)])
            return cos * now, sin * now, 1.0 - (cos + sin) * now

        def write(q, t, value):
            if phase == 0:
                l1[q, t] = value
            else:
                rows = pl.ds(LAST * RPI + q * QUAD * 8 + t, QUAD, stride=8)
                done[rows, :] = value[:QUAD]

        src = (l0, l1)[phase]
        receive(phase, GROUPS)
        return advance(
            phase, GROUPS, src, write, last_halo.at[phase], LAST_PAIRS, coefficients
        )

    def first_step(c, carry):
        group(0, c)
        send_cols(1, c)
        send_rows(1, c)
        return carry

    lax.fori_loop(0, GROUPS, first_step, 0)
    leftover(0)
    send_cols(1, GROUPS)
    send_rows(1, GROUPS)

    sums[...] = jnp.zeros(sums.shape, jnp.float32)

    def second_step(c, carry):
        totals = group(1, c)
        pltpu.make_async_copy(
            done.at[pl.ds(c * RPG, RPG), :], out.at[pl.ds(c * RPG, RPG), :], out_sem.at[c]
        ).start()
        for t in range(8):
            sums[0, t] = sums[0, t] + weight[0, c] * totals[t]
            sums[1, t] = sums[1, t] + weight[1, c] * totals[t]
        return carry

    lax.fori_loop(0, GROUPS, second_step, 0)
    totals = leftover(1)
    store(GROUPS).start()
    for t in range(8):
        rest = jnp.where(sub < QUAD, totals[t], 0.0)
        m0 = sums[0, t] + float(WEIGHT[LAST]) * rest
        m1 = sums[1, t] + float(WEIGHT[LAST] * RATIO[LAST]) * rest
        m0 = jnp.sum(m0, axis=0, keepdims=True)
        m1 = jnp.sum(m1, axis=0, keepdims=True)
        mean_ratio[pl.ds(t, 1), :] = m1 / jnp.maximum(m0, 0.05)

    for phase in range(2):
        for c in range(GROUPS + 1):
            @pl.when(has_north)
            def _():
                rows_to(phase, c, 0, 0).wait_send()
                rows_to(phase, c, 0, 1).wait_send()

            @pl.when(has_south)
            def _():
                rows_to(phase, c, 1, 0).wait_send()
                rows_to(phase, c, 1, 1).wait_send()

            cols_to(phase, c, 0).wait_send()
            cols_to(phase, c, 1).wait_send()
    for c in range(GROUPS + 1):
        store(c).wait()


def source_kernel(
    wind_speed_in, wind_dir_in, ice_in, mean_ratio_in, energy,
    out,
    held, done, wind_speed, wind_dir, ice_mask, mean_ratio, gain,
    in_sem, out_sem, small_sem,
):
    loads = [
        pltpu.make_async_copy(
            energy.at[pl.ds(c * RPC, RPC), :], held.at[pl.ds(c * RPC, RPC), :], in_sem.at[c]
        )
        for c in range(CH)
    ]
    stores = [
        pltpu.make_async_copy(
            done.at[pl.ds(c * RPC, RPC), :], out.at[pl.ds(c * RPC, RPC), :], out_sem.at[c]
        )
        for c in range(CH)
    ]
    smalls = [
        pltpu.make_async_copy(source, target, small_sem.at[n])
        for n, (source, target) in enumerate(
            (
                (wind_dir_in, wind_dir),
                (wind_speed_in, wind_speed),
                (ice_in, ice_mask),
                (mean_ratio_in, mean_ratio),
            )
        )
    ]
    for copy in smalls + loads:
        copy.start()
    for copy in smalls:
        copy.wait()
    ice = ice_mask[...].astype(jnp.float32)
    strength = (1.0 - ice) * 0.05 * wind_speed[...]
    cos_wind = strength * jnp.cos(wind_dir[...])
    sin_wind = strength * jnp.sin(wind_dir[...])
    for d in range(ND):
        gain[pl.ds(8 * d, 8), :] = jnp.maximum(
            float(COS[d]) * cos_wind + float(SIN[d]) * sin_wind, 0.0
        )
    drag = 0.02 * mean_ratio[...]
    cold = 0.7 * ice
    for c in range(CH):
        loads[c].wait()
        losses = [float(RATIO[c * IC + il]) * drag + cold for il in range(IC)]

        def one(d, carry):
            push = gain[pl.ds(pl.multiple_of(8 * d, 8), 8), :]
            for il in range(IC):
                rows = pl.ds(pl.multiple_of((c * IC + il) * RPI + 8 * d, 8), 8)
                net = float(RATIO[c * IC + il]) * push - losses[il]
                done[rows, :] = held[rows, :] * jnp.exp(net)
            return carry

        lax.fori_loop(0, ND, one, 0, unroll=8)
        stores[c].start()
    for copy in stores:
        copy.wait()


def to_tiles(x):
    lead, rows, cols = x.shape
    x = x.reshape(lead, rows, cols // 128, 128).transpose(0, 2, 1, 3)
    return x.reshape(lead * rows * cols // 128, 128)


def from_tiles(x, shape):
    lead, rows, cols = shape
    x = x.reshape(lead, cols // 128, rows, 128).transpose(0, 2, 1, 3)
    return x.reshape(shape)


def on_device(n_strip, n_pt, spectra, courant, wind_speed, wind_dir, sea_mask, ice_mask):
    total = spectra.shape[0] * 8
    vmem = pl.BlockSpec(memory_space=pltpu.VMEM)
    hbm = pl.BlockSpec(memory_space=pl.ANY)
    sem = pltpu.SemaphoreType.DMA
    whole = jax.ShapeDtypeStruct((total, 128), jnp.float32)
    blocks = pltpu.VMEM((GROUPS, ND, 8, 8, 128), jnp.float32)
    last_blocks = pltpu.VMEM((4, 8, 8, 128), jnp.float32)
    energy, mean_ratio = pl.pallas_call(
        functools.partial(kernel, n_strip, n_pt),
        out_shape=[
            whole,
            jax.ShapeDtypeStruct((8, 128), jnp.float32),
        ],
        in_specs=[hbm] * 3,
        out_specs=[hbm, vmem],
        scratch_shapes=[
            pltpu.VMEM((total + 16, 128), jnp.float32),
            pltpu.VMEM((total, 128), jnp.float32),
            blocks,
            blocks,
            last_blocks,
            last_blocks,
            pltpu.VMEM((8, 128), jnp.int32),
            pltpu.VMEM((8, 8, 128), jnp.float32),
            pltpu.SMEM((NF,), jnp.float32),
            pltpu.VMEM((GROUPS, 8, 128), jnp.float32),
            pltpu.VMEM((2, GROUPS, 8, 128), jnp.float32),
            pltpu.VMEM((2, 8, 8, 128), jnp.float32),
            pltpu.VMEM((2, GROUPS, 2, 2, HALF, 8, 128), jnp.float32),
            pltpu.VMEM((2, 2, 2, 2, 8, 128), jnp.float32),
            pltpu.VMEM((2, GROUPS + 1, 8, 128), jnp.float32),
            pltpu.VMEM((2, GROUPS + 1, 2, 8, 128), jnp.float32),
            sem((GROUPS + 1,)),
            sem((GROUPS + 1,)),
            sem((2,)),
            sem((2, GROUPS + 1, 2, 2)),
            sem((2, GROUPS + 1, 2, 2)),
            sem((2, GROUPS + 1, 2)),
            sem((2, GROUPS + 1, 2)),
        ],
        compiler_params=pltpu.CompilerParams(
            collective_id=0, has_side_effects=True, vmem_limit_bytes=60 * 1024 * 1024
        ),
        cost_estimate=pl.CostEstimate(
            flops=16 * total * 128, bytes_accessed=8 * total * 128, transcendentals=0
        ),
    )(courant, to_tiles(sea_mask[None]), to_tiles(spectra))
    result = pl.pallas_call(
        source_kernel,
        out_shape=whole,
        in_specs=[hbm] * 5,
        out_specs=hbm,
        scratch_shapes=[
            pltpu.VMEM((total, 128), jnp.float32),
            pltpu.VMEM((total, 128), jnp.float32),
            pltpu.VMEM((8, 128), jnp.float32),
            pltpu.VMEM((8, 128), jnp.float32),
            pltpu.VMEM((8, 128), jnp.int32),
            pltpu.VMEM((8, 128), jnp.float32),
            pltpu.VMEM((ND * 8, 128), jnp.float32),
            sem((CH,)),
            sem((CH,)),
            sem((4,)),
        ],
        compiler_params=pltpu.CompilerParams(vmem_limit_bytes=60 * 1024 * 1024),
        cost_estimate=pl.CostEstimate(
            flops=4 * total * 128, bytes_accessed=8 * total * 128, transcendentals=total * 128
        ),
    )(
        to_tiles(wind_speed[None]),
        to_tiles(wind_dir[None]),
        to_tiles(ice_mask[None]),
        mean_ratio,
        energy,
    )
    return from_tiles(result, spectra.shape)


def solution(mesh):
    in_specs = (
        P(None, "strip", "pt"),
        P(),
        P("strip", "pt"),
        P("strip", "pt"),
        P("strip", "pt"),
        P("strip", "pt"),
    )
    return jax.shard_map(
        functools.partial(on_device, mesh.shape["strip"], mesh.shape["pt"]),
        mesh=mesh,
        in_specs=in_specs,
        out_specs=P(None, "strip", "pt"),
        check_vma=False,
    )
```

```python
import functools
import numpy as np
import jax
import jax.numpy as jnp
from jax import lax
from jax.experimental import pallas as pl
from jax.experimental.pallas import tpu as pltpu
from jax.sharding import PartitionSpec as P

NF = 25
ND = 24
HALF = ND // 2
CH = 5
IC = NF // CH
RPI = ND * 8
RPC = RPI * IC
MESH = pl.DeviceIdType.MESH

THETA = (np.float32(2.0 * np.pi) * np.arange(ND, dtype=np.float32) / np.float32(ND)).astype(np.float32)
COS = np.cos(THETA).astype(np.float32)
SIN = np.sin(THETA).astype(np.float32)
RATIO = np.float32(1.1) ** np.arange(NF, dtype=np.float32)
WEIGHT = (RATIO / (ND * np.sum(RATIO, dtype=np.float64))).astype(np.float32)
FROM_WEST = [d for d in range(ND) if COS[d] > 0.0]
FROM_EAST = [d for d in range(ND) if not COS[d] > 0.0]


def pieces():
    return ((0, 0, 8, 0), (0, 8, 4, 8), (1, 0, 4, 12), (1, 4, 8, 16))


def kernel(
    n_strip, n_pt,
    courant_in, sea_in, spectra,
    out, mean_ratio,
    e0, e1, sea_mask, sea, courant, table, rise,
    row_send, row_recv, col_send, col_recv, corner_recv, turn,
    in_sem, out_sem, small_sem, send_sem, recv_sem, corner_send_sem, corner_recv_sem,
):
    s = lax.axis_index("strip")
    p = lax.axis_index("pt")
    east = lax.rem(p + 1, n_pt)
    west = lax.rem(p + n_pt - 1, n_pt)
    has_south = s > 0
    has_north = s < n_strip - 1

    def load(c):
        rows = pl.ds(pl.multiple_of(c * RPC, RPC), RPC)
        return pltpu.make_async_copy(spectra.at[rows, :], e0.at[rows, :], in_sem.at[c])

    def store(c):
        rows = pl.ds(pl.multiple_of(c * RPC, RPC), RPC)
        return pltpu.make_async_copy(e0.at[rows, :], out.at[rows, :], out_sem.at[c])

    def rows_to(phase, c, way):
        return pltpu.make_async_remote_copy(
            src_ref=row_send.at[phase, c, way],
            dst_ref=row_recv.at[phase, c, way],
            send_sem=send_sem.at[phase, c, way],
            recv_sem=recv_sem.at[phase, c, way],
            device_id={"strip": s + 1 if way == 0 else s - 1},
            device_id_type=MESH,
        )

    def cols_to(phase, c, way):
        return pltpu.make_async_remote_copy(
            src_ref=col_send.at[phase, c],
            dst_ref=col_recv.at[phase, c, way],
            send_sem=send_sem.at[phase, c, 2 + way],
            recv_sem=recv_sem.at[phase, c, 2 + way],
            device_id={"pt": east if way == 0 else west},
            device_id_type=MESH,
        )

    def corners_to(c, way):
        return pltpu.make_async_remote_copy(
            src_ref=col_send.at[0, c],
            dst_ref=corner_recv.at[c, way],
            send_sem=corner_send_sem.at[c, way],
            recv_sem=corner_recv_sem.at[c, way],
            device_id={"strip": s + 1 if way == 0 else s - 1},
            device_id_type=MESH,
        )

    def send_corners(c):
        @pl.when(has_north)
        def _():
            corners_to(c, 0).start()

        @pl.when(has_south)
        def _():
            corners_to(c, 1).start()

    def receive_corners(c):
        @pl.when(has_south)
        def _():
            corners_to(c, 0).wait_recv()

        @pl.when(has_north)
        def _():
            corners_to(c, 1).wait_recv()

    def send_rows(phase, c):
        @pl.when(has_north)
        def _():
            rows_to(phase, c, 0).start()

        @pl.when(has_south)
        def _():
            rows_to(phase, c, 1).start()

    def send_cols(phase, c):
        cols_to(phase, c, 0).start()
        cols_to(phase, c, 1).start()

    def receive_rows(phase, c):
        @pl.when(has_south)
        def _():
            rows_to(phase, c, 0).wait_recv()

        @pl.when(has_north)
        def _():
            rows_to(phase, c, 1).wait_recv()

    def receive_cols(phase, c):
        cols_to(phase, c, 0).wait_recv()
        cols_to(phase, c, 1).wait_recv()

    smalls = [
        pltpu.make_async_copy(source, target, small_sem.at[n])
        for n, (source, target) in enumerate(
            ((courant_in, courant), (sea_in, sea_mask))
        )
    ]
    for c in range(CH):
        load(c).start()
    for small in smalls:
        small.start()

    barrier = pltpu.get_barrier_semaphore()
    for side in (east, west):
        pl.semaphore_signal(barrier, inc=1, device_id={"pt": side}, device_id_type=MESH)

    @pl.when(has_north)
    def _():
        pl.semaphore_signal(barrier, inc=1, device_id={"strip": s + 1}, device_id_type=MESH)

    @pl.when(has_south)
    def _():
        pl.semaphore_signal(barrier, inc=1, device_id={"strip": s - 1}, device_id_type=MESH)

    @pl.when(jnp.logical_not(has_south))
    def _():
        row_recv[:, :, 0] = jnp.zeros(row_recv.shape[:2] + row_recv.shape[3:], jnp.float32)
        corner_recv[:, 0] = jnp.zeros((CH, 8, 128), jnp.float32)

    @pl.when(jnp.logical_not(has_north))
    def _():
        row_recv[:, :, 1] = jnp.zeros(row_recv.shape[:2] + row_recv.shape[3:], jnp.float32)
        corner_recv[:, 1] = jnp.zeros((CH, 8, 128), jnp.float32)

    for i in range(NF):
        table[0, i] = float(WEIGHT[i])
        table[1, i] = float(WEIGHT[i] * RATIO[i])
    for d in range(HALF):
        rise[pl.ds(d, 1), :] = jnp.full((1, 128), float(abs(SIN[d])), jnp.float32)
        rise[pl.ds(16 + d, 1), :] = jnp.full((1, 128), float(abs(SIN[HALF + d])), jnp.float32)
    lane = lax.broadcasted_iota(jnp.int32, (8, 128), 1)
    sub = lax.broadcasted_iota(jnp.int32, (8, 128), 0)
    low = sub < 4
    first_lane = lane == 0
    last_lane = lane == 127

    def pack_rows(src, phase, c):
        def one(il, carry):
            base = pl.multiple_of((c * IC + il) * RPI, 8)
            to = pl.multiple_of(il * ND, 8)
            for tile, first, count, at in pieces():
                up = src[pl.ds(base + first * 8 + 3 + 4 * tile, count, stride=8), :]
                row_send[phase, c, 0, pl.ds(to + at, count), :] = up
                down = src[pl.ds(base + (HALF + first) * 8 + 4 * tile, count, stride=8), :]
                row_send[phase, c, 1, pl.ds(to + at, count), :] = down
            return carry

        lax.fori_loop(0, IC, one, 0, unroll=True)

    spot = jnp.where(low, lane - 1, lane)
    pair = lax.rem(spot, HALF)
    south = pair < HALF // 2

    def put(acc, n, pos, neg):
        mixed = pltpu.roll(jnp.where(low, neg, pos), n + 1, 1)
        return jnp.where(spot == n, mixed, acc)

    def pack_cols(src, phase, c):
        base = pl.multiple_of(c * RPC, 8)
        acc = jnp.zeros((8, 128), jnp.float32)
        for il in range(IC):
            for m in range(HALF):
                pos = src[pl.ds(base + il * RPI + 8 * FROM_WEST[m], 8), :]
                neg = src[pl.ds(base + il * RPI + 8 * FROM_EAST[m], 8), :]
                acc = put(acc, il * HALF + m, pos, neg)
        col_send[phase, c] = acc

    load(0).wait()
    pack_cols(e0, 0, 0)
    pack_rows(e0, 0, 0)
    pl.semaphore_wait(
        barrier, 2 + has_north.astype(jnp.int32) + has_south.astype(jnp.int32)
    )
    send_cols(0, 0)
    send_corners(0)
    send_rows(0, 0)

    def first_halo(c, carry):
        load(c).wait()
        pack_cols(e0, 0, c)
        send_cols(0, c)
        send_corners(c)
        pack_rows(e0, 0, c)
        send_rows(0, c)
        return carry

    lax.fori_loop(1, CH, first_halo, 0)
    for small in smalls:
        small.wait()
    sea_all = sea_mask[...].astype(jnp.float32)
    sea[...] = sea_all
    slope = jnp.zeros((8, 128), jnp.float32)
    for m in range(HALF):
        here = jnp.where(low, float(abs(SIN[FROM_EAST[m]])), float(abs(SIN[FROM_WEST[m]])))
        slope = jnp.where(pair == m, here, slope)
    edge_row = lax.rem(sub, 4) == jnp.where(south, 0, 3)
    used = edge_row & (spot >= 0) & (spot < IC * HALF)
    shore = jnp.where(
        low,
        jnp.broadcast_to(sea_all[:, 0:1], (8, 128)),
        jnp.broadcast_to(sea_all[:, 127:128], (8, 128)),
    )
    turn[...] = jnp.where(used, slope * shore, 0.0)

    def advance(src, dst, phase, c, sums):
        receive_cols(phase, c)
        if phase == 1:
            receive_rows(phase, c)
        halo = jnp.where(low, col_recv[phase, c, 1], pltpu.roll(col_recv[phase, c, 0], 2, 1))
        halo = pltpu.roll(halo, 4, 0)
        sea_now = sea[...]
        acc = jnp.zeros((8, 128), jnp.float32)
        m0, m1 = sums
        chunk = pl.multiple_of(c * RPC, 8)
        for il in range(IC):
            i = c * IC + il
            base = chunk + il * RPI
            at = il * ND
            speed = courant[i] * sea_now
            keep = [sea_now - speed * float(k) for k in (np.abs(COS[:4]) + np.abs(SIN[:4]))]
            total = jnp.zeros((8, 128), jnp.float32)

            def step(d, core, side):
                if d < HALF:
                    near = pltpu.roll(core, 1, 0)
                    r0, r1, way, m = 0, 4, 0, d
                else:
                    near = pltpu.roll(core, 7, 0)
                    r0, r1, way, m = 3, 7, 1, d - HALF
                if phase == 0:
                    near = jnp.where((sub == r0) | (sub == r1), 0.0, near)
                else:
                    h0 = row_recv[phase, c, way, pl.ds(at + m, 1), :]
                    h1 = row_recv[phase, c, way, pl.ds(at + HALF + m, 1), :]
                    near = jnp.where(sub == r0, h0, jnp.where(sub == r1, h1, near))
                flow = float(abs(COS[d])) * side + float(abs(SIN[d])) * near
                q = d % 6
                fresh = keep[q if q < 4 else 6 - q] * core + speed * flow
                dst[pl.ds(base + 8 * d, 8), :] = fresh
                return fresh

            for m in range(HALF):
                pos = src[pl.ds(base + 8 * FROM_WEST[m], 8), :]
                neg = src[pl.ds(base + 8 * FROM_EAST[m], 8), :]
                n = il * HALF + m
                edge = pltpu.roll(halo, 126 - n, 1)
                rolled_pos = pltpu.roll(pos, 1, 1)
                rolled_neg = pltpu.roll(neg, 127, 1)
                swap = pltpu.roll(jnp.where(first_lane, rolled_pos, rolled_neg), 4, 0)
                side_pos = jnp.where(first_lane, jnp.where(low, edge, swap), rolled_pos)
                side_neg = jnp.where(last_lane, jnp.where(low, swap, edge), rolled_neg)
                new_pos = step(FROM_WEST[m], pos, side_pos)
                new_neg = step(FROM_EAST[m], neg, side_neg)
                if phase == 0:
                    acc = put(acc, n, new_pos, new_neg)
                else:
                    total = total + (new_pos + new_neg)
            if phase == 1:
                m0 = m0 + table[0, i] * total
                m1 = m1 + table[1, i] * total
        if phase == 0:
            receive_corners(c)
            rate = jnp.zeros((8, 128), jnp.float32)
            for il in range(IC):
                inside = (spot >= il * HALF) & (spot < (il + 1) * HALF)
                rate = jnp.where(inside, courant[c * IC + il], rate)
            corner = jnp.where(
                south,
                pltpu.roll(corner_recv[c, 0], 5, 0),
                pltpu.roll(corner_recv[c, 1], 3, 0),
            )
            col_send[1, c] = acc + rate * (turn[...] * corner)
        return m0, m1

    zero = jnp.zeros((8, 128), jnp.float32)

    def first_step(c, carry):
        advance(e0, e1, 0, c, (zero, zero))
        send_cols(1, c)
        pack_rows(e1, 1, c)
        send_rows(1, c)
        return carry

    lax.fori_loop(0, CH, first_step, 0)

    def first_edge(c):
        receive_rows(0, c)

        def one(il, carry):
            i = c * IC + il
            base = pl.multiple_of(i * RPI, 8)
            at = pl.multiple_of(il * ND, 8)
            for way in range(2):
                for tile, first, count, to in pieces():
                    row = 4 * tile + 3 * way
                    rows = pl.ds(base + (HALF * way + first) * 8 + row, count, stride=8)
                    speed = courant[i] * sea[pl.ds(row, 1), :]
                    term = row_recv[0, c, way, pl.ds(at + to, count), :]
                    term = term * rise[pl.ds(16 * way + first, count), :]
                    e1[rows, :] = e1[rows, :] + speed * term
            return carry

        lax.fori_loop(0, IC, one, 0, unroll=True)

    def second_step(c, sums):
        first_edge(c)
        sums = advance(e1, e0, 1, c, sums)
        store(c).start()
        return sums

    m0, m1 = lax.fori_loop(0, CH, second_step, (zero, zero))
    mean_ratio[...] = m1 / jnp.maximum(m0, 0.05)

    def finish(c, carry):
        for phase in range(2):
            @pl.when(has_north)
            def _():
                rows_to(phase, c, 0).wait_send()

            @pl.when(has_south)
            def _():
                rows_to(phase, c, 1).wait_send()

            cols_to(phase, c, 0).wait_send()
            cols_to(phase, c, 1).wait_send()

        @pl.when(has_north)
        def _():
            corners_to(c, 0).wait_send()

        @pl.when(has_south)
        def _():
            corners_to(c, 1).wait_send()

        store(c).wait()
        return carry

    lax.fori_loop(0, CH, finish, 0)


def source_kernel(
    wind_speed_in, wind_dir_in, ice_in, mean_ratio_in, energy,
    out,
    held, done, wind_speed, wind_dir, ice_mask, mean_ratio, gain,
    in_sem, out_sem, small_sem,
):
    loads = [
        pltpu.make_async_copy(
            energy.at[pl.ds(c * RPC, RPC), :], held.at[pl.ds(c * RPC, RPC), :], in_sem.at[c]
        )
        for c in range(CH)
    ]
    stores = [
        pltpu.make_async_copy(
            done.at[pl.ds(c * RPC, RPC), :], out.at[pl.ds(c * RPC, RPC), :], out_sem.at[c]
        )
        for c in range(CH)
    ]
    smalls = [
        pltpu.make_async_copy(source, target, small_sem.at[n])
        for n, (source, target) in enumerate(
            (
                (wind_dir_in, wind_dir),
                (wind_speed_in, wind_speed),
                (ice_in, ice_mask),
                (mean_ratio_in, mean_ratio),
            )
        )
    ]
    for copy in smalls + loads:
        copy.start()
    for copy in smalls:
        copy.wait()
    ice = ice_mask[...].astype(jnp.float32)
    strength = (1.0 - ice) * 0.05 * wind_speed[...]
    cos_wind = strength * jnp.cos(wind_dir[...])
    sin_wind = strength * jnp.sin(wind_dir[...])
    for d in range(ND):
        gain[pl.ds(8 * d, 8), :] = jnp.maximum(
            float(COS[d]) * cos_wind + float(SIN[d]) * sin_wind, 0.0
        )
    drag = 0.02 * mean_ratio[...]
    cold = 0.7 * ice
    for c in range(CH):
        loads[c].wait()
        losses = [float(RATIO[c * IC + il]) * drag + cold for il in range(IC)]

        def one(d, carry):
            push = gain[pl.ds(pl.multiple_of(8 * d, 8), 8), :]
            for il in range(IC):
                rows = pl.ds(pl.multiple_of((c * IC + il) * RPI + 8 * d, 8), 8)
                net = float(RATIO[c * IC + il]) * push - losses[il]
                done[rows, :] = held[rows, :] * jnp.exp(net)
            return carry

        lax.fori_loop(0, ND, one, 0, unroll=8)
        stores[c].start()
    for copy in stores:
        copy.wait()


def to_tiles(x):
    lead, rows, cols = x.shape
    x = x.reshape(lead, rows, cols // 128, 128).transpose(0, 2, 1, 3)
    return x.reshape(lead * rows * cols // 128, 128)


def from_tiles(x, shape):
    lead, rows, cols = shape
    x = x.reshape(lead, cols // 128, rows, 128).transpose(0, 2, 1, 3)
    return x.reshape(shape)


def on_device(n_strip, n_pt, spectra, courant, wind_speed, wind_dir, sea_mask, ice_mask):
    total = spectra.shape[0] * 8
    vmem = pl.BlockSpec(memory_space=pltpu.VMEM)
    hbm = pl.BlockSpec(memory_space=pl.ANY)
    sem = pltpu.SemaphoreType.DMA
    rows = IC * ND
    whole = jax.ShapeDtypeStruct((total, 128), jnp.float32)
    point = jax.ShapeDtypeStruct((8, 128), jnp.float32)
    energy, mean_ratio = pl.pallas_call(
        functools.partial(kernel, n_strip, n_pt),
        out_shape=[whole, point],
        in_specs=[hbm] * 3,
        out_specs=[hbm, vmem],
        scratch_shapes=[
            pltpu.VMEM((total, 128), jnp.float32),
            pltpu.VMEM((total, 128), jnp.float32),
            pltpu.VMEM((8, 128), jnp.int32),
            pltpu.VMEM((8, 128), jnp.float32),
            pltpu.SMEM((NF,), jnp.float32),
            pltpu.SMEM((2, NF), jnp.float32),
            pltpu.VMEM((32, 128), jnp.float32),
            pltpu.VMEM((2, CH, 2, rows, 128), jnp.float32),
            pltpu.VMEM((2, CH, 2, rows, 128), jnp.float32),
            pltpu.VMEM((2, CH, 8, 128), jnp.float32),
            pltpu.VMEM((2, CH, 2, 8, 128), jnp.float32),
            pltpu.VMEM((CH, 2, 8, 128), jnp.float32),
            pltpu.VMEM((8, 128), jnp.float32),
            sem((CH,)),
            sem((CH,)),
            sem((2,)),
            sem((2, CH, 4)),
            sem((2, CH, 4)),
            sem((CH, 2)),
            sem((CH, 2)),
        ],
        compiler_params=pltpu.CompilerParams(
            collective_id=0, has_side_effects=True, vmem_limit_bytes=60 * 1024 * 1024
        ),
        cost_estimate=pl.CostEstimate(
            flops=30 * total * 128, bytes_accessed=8 * total * 128, transcendentals=0
        ),
    )(courant, to_tiles(sea_mask[None]), to_tiles(spectra))
    result = pl.pallas_call(
        source_kernel,
        out_shape=whole,
        in_specs=[hbm] * 5,
        out_specs=hbm,
        scratch_shapes=[
            pltpu.VMEM((total, 128), jnp.float32),
            pltpu.VMEM((total, 128), jnp.float32),
            pltpu.VMEM((8, 128), jnp.float32),
            pltpu.VMEM((8, 128), jnp.float32),
            pltpu.VMEM((8, 128), jnp.int32),
            pltpu.VMEM((8, 128), jnp.float32),
            pltpu.VMEM((ND * 8, 128), jnp.float32),
            sem((CH,)),
            sem((CH,)),
            sem((4,)),
        ],
        compiler_params=pltpu.CompilerParams(vmem_limit_bytes=60 * 1024 * 1024),
        cost_estimate=pl.CostEstimate(
            flops=4 * total * 128, bytes_accessed=8 * total * 128, transcendentals=total * 128
        ),
    )(
        to_tiles(wind_speed[None]),
        to_tiles(wind_dir[None]),
        to_tiles(ice_mask[None]),
        mean_ratio,
        energy,
    )
    return from_tiles(result, spectra.shape)


def solution(mesh):
    in_specs = (
        P(None, "strip", "pt"),
        P(),
        P("strip", "pt"),
        P("strip", "pt"),
        P("strip", "pt"),
        P("strip", "pt"),
    )
    return jax.shard_map(
        functools.partial(on_device, mesh.shape["strip"], mesh.shape["pt"]),
        mesh=mesh,
        in_specs=in_specs,
        out_specs=P(None, "strip", "pt"),
        check_vma=False,
    )
```

```python
import functools
import numpy as np
import jax
import jax.numpy as jnp
from jax import lax
from jax.experimental import pallas as pl
from jax.experimental.pallas import tpu as pltpu
from jax.sharding import PartitionSpec as P

NF = 25
ND = 24
HALF = ND // 2
CH = 5
IC = NF // CH
RPI = ND * 8
RPC = RPI * IC
MESH = pl.DeviceIdType.MESH

THETA = (np.float32(2.0 * np.pi) * np.arange(ND, dtype=np.float32) / np.float32(ND)).astype(np.float32)
COS = np.cos(THETA).astype(np.float32)
SIN = np.sin(THETA).astype(np.float32)
RATIO = np.float32(1.1) ** np.arange(NF, dtype=np.float32)
WEIGHT = (RATIO / (ND * np.sum(RATIO, dtype=np.float64))).astype(np.float32)
FROM_WEST = [d for d in range(ND) if COS[d] > 0.0]
FROM_EAST = [d for d in range(ND) if not COS[d] > 0.0]


def pieces():
    return ((0, 0, 8, 0), (0, 8, 4, 8), (1, 0, 4, 12), (1, 4, 8, 16))


def kernel(
    n_strip, n_pt,
    courant_in, sea_in, wind_speed_in, wind_dir_in, ice_in, spectra,
    out, mean_out, gain_out,
    e0, e1, sea_mask, sea, courant, table, wind_speed, wind_dir, ice_mask,
    row_send, row_recv, col_send, col_recv, gain, mean,
    in_sem, out_sem, small_sem, send_sem, recv_sem,
):
    s = lax.axis_index("strip")
    p = lax.axis_index("pt")
    east = lax.rem(p + 1, n_pt)
    west = lax.rem(p + n_pt - 1, n_pt)
    has_south = s > 0
    has_north = s < n_strip - 1

    def load(c):
        rows = pl.ds(pl.multiple_of(c * RPC, RPC), RPC)
        return pltpu.make_async_copy(spectra.at[rows, :], e0.at[rows, :], in_sem.at[c])

    def store(c):
        rows = pl.ds(pl.multiple_of(c * RPC, RPC), RPC)
        return pltpu.make_async_copy(e0.at[rows, :], out.at[rows, :], out_sem.at[c])

    def rows_to(phase, c, way):
        return pltpu.make_async_remote_copy(
            src_ref=row_send.at[phase, c, way],
            dst_ref=row_recv.at[phase, c, way],
            send_sem=send_sem.at[phase, c, way],
            recv_sem=recv_sem.at[phase, c, way],
            device_id={"strip": s + 1 if way == 0 else s - 1},
            device_id_type=MESH,
        )

    def cols_to(phase, c, way):
        return pltpu.make_async_remote_copy(
            src_ref=col_send.at[phase, c],
            dst_ref=col_recv.at[phase, c, way],
            send_sem=send_sem.at[phase, c, 2 + way],
            recv_sem=recv_sem.at[phase, c, 2 + way],
            device_id={"pt": east if way == 0 else west},
            device_id_type=MESH,
        )

    def send_rows(phase, c):
        @pl.when(has_north)
        def _():
            rows_to(phase, c, 0).start()

        @pl.when(has_south)
        def _():
            rows_to(phase, c, 1).start()

    def send_cols(phase, c):
        cols_to(phase, c, 0).start()
        cols_to(phase, c, 1).start()

    def receive_rows(phase, c):
        @pl.when(has_south)
        def _():
            rows_to(phase, c, 0).wait_recv()

        @pl.when(has_north)
        def _():
            rows_to(phase, c, 1).wait_recv()

    def receive_cols(phase, c):
        cols_to(phase, c, 0).wait_recv()
        cols_to(phase, c, 1).wait_recv()

    smalls = [
        pltpu.make_async_copy(source, target, small_sem.at[n])
        for n, (source, target) in enumerate(
            (
                (courant_in, courant),
                (sea_in, sea_mask),
                (wind_speed_in, wind_speed),
                (wind_dir_in, wind_dir),
                (ice_in, ice_mask),
            )
        )
    ]
    for c in range(CH):
        load(c).start()
    for small in smalls:
        small.start()

    barrier = pltpu.get_barrier_semaphore()
    for side in (east, west):
        pl.semaphore_signal(barrier, inc=1, device_id={"pt": side}, device_id_type=MESH)

    @pl.when(has_north)
    def _():
        pl.semaphore_signal(barrier, inc=1, device_id={"strip": s + 1}, device_id_type=MESH)

    @pl.when(has_south)
    def _():
        pl.semaphore_signal(barrier, inc=1, device_id={"strip": s - 1}, device_id_type=MESH)

    @pl.when(jnp.logical_not(has_south))
    def _():
        row_recv[:, :, 0] = jnp.zeros(row_recv.shape[:2] + row_recv.shape[3:], jnp.float32)

    @pl.when(jnp.logical_not(has_north))
    def _():
        row_recv[:, :, 1] = jnp.zeros(row_recv.shape[:2] + row_recv.shape[3:], jnp.float32)

    for i in range(NF):
        table[0, i] = float(WEIGHT[i])
        table[1, i] = float(WEIGHT[i] * RATIO[i])
    lane = lax.broadcasted_iota(jnp.int32, (8, 128), 1)
    sub = lax.broadcasted_iota(jnp.int32, (8, 128), 0)
    low = sub < 4
    first_lane = lane == 0
    last_lane = lane == 127

    def pack_rows(src, phase, c):
        def one(il, carry):
            base = pl.multiple_of((c * IC + il) * RPI, 8)
            to = pl.multiple_of(il * ND, 8)
            for tile, first, count, at in pieces():
                up = src[pl.ds(base + first * 8 + 3 + 4 * tile, count, stride=8), :]
                row_send[phase, c, 0, pl.ds(to + at, count), :] = up
                down = src[pl.ds(base + (HALF + first) * 8 + 4 * tile, count, stride=8), :]
                row_send[phase, c, 1, pl.ds(to + at, count), :] = down
            return carry

        lax.fori_loop(0, IC, one, 0, unroll=True)

    spot = jnp.where(low, lane - 1, lane)

    def put(acc, n, pos, neg):
        mixed = pltpu.roll(jnp.where(low, neg, pos), n + 1, 1)
        return jnp.where(spot == n, mixed, acc)

    def pack_cols(src, phase, c):
        base = pl.multiple_of(c * RPC, 8)
        acc = jnp.zeros((8, 128), jnp.float32)
        for il in range(IC):
            for m in range(HALF):
                pos = src[pl.ds(base + il * RPI + 8 * FROM_WEST[m], 8), :]
                neg = src[pl.ds(base + il * RPI + 8 * FROM_EAST[m], 8), :]
                acc = put(acc, il * HALF + m, pos, neg)
        col_send[phase, c] = acc

    load(0).wait()
    pack_rows(e0, 0, 0)
    pl.semaphore_wait(
        barrier, 2 + has_north.astype(jnp.int32) + has_south.astype(jnp.int32)
    )
    send_rows(0, 0)
    pack_cols(e0, 0, 0)
    send_cols(0, 0)

    def first_halo(c, carry):
        load(c).wait()
        pack_rows(e0, 0, c)
        send_rows(0, c)
        pack_cols(e0, 0, c)
        send_cols(0, c)
        return carry

    lax.fori_loop(1, CH, first_halo, 0)
    for small in smalls:
        small.wait()
    sea[...] = sea_mask[...].astype(jnp.float32)

    strength = (1.0 - ice_mask[...].astype(jnp.float32)) * 0.05 * wind_speed[...]
    cos_wind = strength * jnp.cos(wind_dir[...])
    sin_wind = strength * jnp.sin(wind_dir[...])
    for d in range(ND):
        gain[pl.ds(8 * d, 8), :] = jnp.maximum(
            float(COS[d]) * cos_wind + float(SIN[d]) * sin_wind, 0.0
        )
    gain_copy = pltpu.make_async_copy(gain, gain_out, small_sem.at[0])
    gain_copy.start()

    def advance(src, dst, phase, c, sums):
        receive_cols(phase, c)
        receive_rows(phase, c)
        halo = jnp.where(low, col_recv[phase, c, 1], pltpu.roll(col_recv[phase, c, 0], 2, 1))
        halo = pltpu.roll(halo, 4, 0)
        sea_now = sea[...]
        acc = jnp.zeros((8, 128), jnp.float32)
        m0, m1 = sums
        chunk = pl.multiple_of(c * RPC, 8)
        for il in range(IC):
            i = c * IC + il
            base = chunk + il * RPI
            at = il * ND
            speed = courant[i] * sea_now
            keep = [sea_now - speed * float(k) for k in (np.abs(COS[:4]) + np.abs(SIN[:4]))]
            total = jnp.zeros((8, 128), jnp.float32)

            def step(d, core, side):
                if d < HALF:
                    near = pltpu.roll(core, 1, 0)
                    r0, r1, way, m = 0, 4, 0, d
                else:
                    near = pltpu.roll(core, 7, 0)
                    r0, r1, way, m = 3, 7, 1, d - HALF
                h0 = row_recv[phase, c, way, pl.ds(at + m, 1), :]
                h1 = row_recv[phase, c, way, pl.ds(at + HALF + m, 1), :]
                near = jnp.where(sub == r0, h0, jnp.where(sub == r1, h1, near))
                flow = float(abs(COS[d])) * side + float(abs(SIN[d])) * near
                q = d % 6
                fresh = keep[q if q < 4 else 6 - q] * core + speed * flow
                dst[pl.ds(base + 8 * d, 8), :] = fresh
                return fresh

            for m in range(HALF):
                pos = src[pl.ds(base + 8 * FROM_WEST[m], 8), :]
                neg = src[pl.ds(base + 8 * FROM_EAST[m], 8), :]
                n = il * HALF + m
                edge = pltpu.roll(halo, 126 - n, 1)
                rolled_pos = pltpu.roll(pos, 1, 1)
                rolled_neg = pltpu.roll(neg, 127, 1)
                swap = pltpu.roll(jnp.where(first_lane, rolled_pos, rolled_neg), 4, 0)
                side_pos = jnp.where(first_lane, jnp.where(low, edge, swap), rolled_pos)
                side_neg = jnp.where(last_lane, jnp.where(low, swap, edge), rolled_neg)
                new_pos = step(FROM_WEST[m], pos, side_pos)
                new_neg = step(FROM_EAST[m], neg, side_neg)
                if phase == 0:
                    acc = put(acc, n, new_pos, new_neg)
                else:
                    total = total + (new_pos + new_neg)
            if phase == 1:
                m0 = m0 + table[0, i] * total
                m1 = m1 + table[1, i] * total
        if phase == 0:
            col_send[1, c] = acc
        return m0, m1

    zero = jnp.zeros((8, 128), jnp.float32)

    def first_step(c, carry):
        advance(e0, e1, 0, c, (zero, zero))
        send_cols(1, c)
        pack_rows(e1, 1, c)
        send_rows(1, c)
        return carry

    lax.fori_loop(0, CH, first_step, 0)

    def second_step(c, sums):
        sums = advance(e1, e0, 1, c, sums)
        store(c).start()
        return sums

    m0, m1 = lax.fori_loop(0, CH, second_step, (zero, zero))
    mean[...] = m1 / jnp.maximum(m0, 0.05)
    mean_copy = pltpu.make_async_copy(mean, mean_out, small_sem.at[1])
    mean_copy.start()

    def finish(c, carry):
        for phase in range(2):
            @pl.when(has_north)
            def _():
                rows_to(phase, c, 0).wait_send()

            @pl.when(has_south)
            def _():
                rows_to(phase, c, 1).wait_send()

            cols_to(phase, c, 0).wait_send()
            cols_to(phase, c, 1).wait_send()

        store(c).wait()
        return carry

    lax.fori_loop(0, CH, finish, 0)
    gain_copy.wait()
    mean_copy.wait()


def source_kernel(
    gain_in, ice_in, mean_ratio_in, energy,
    out,
    held, done, gain, ice_mask, mean_ratio,
    in_sem, out_sem, small_sem,
):
    loads = [
        pltpu.make_async_copy(
            energy.at[pl.ds(c * RPC, RPC), :], held.at[pl.ds(c * RPC, RPC), :], in_sem.at[c]
        )
        for c in range(CH)
    ]
    stores = [
        pltpu.make_async_copy(
            done.at[pl.ds(c * RPC, RPC), :], out.at[pl.ds(c * RPC, RPC), :], out_sem.at[c]
        )
        for c in range(CH)
    ]
    smalls = [
        pltpu.make_async_copy(source, target, small_sem.at[n])
        for n, (source, target) in enumerate(
            (
                (mean_ratio_in, mean_ratio),
                (ice_in, ice_mask),
                (gain_in, gain),
            )
        )
    ]
    for copy in smalls + loads:
        copy.start()
    for copy in smalls:
        copy.wait()
    ice = ice_mask[...].astype(jnp.float32)
    drag = 0.02 * mean_ratio[...]
    cold = 0.7 * ice
    for c in range(CH):
        loads[c].wait()
        losses = [float(RATIO[c * IC + il]) * drag + cold for il in range(IC)]

        def one(d, carry):
            push = gain[pl.ds(pl.multiple_of(8 * d, 8), 8), :]
            for il in range(IC):
                rows = pl.ds(pl.multiple_of((c * IC + il) * RPI + 8 * d, 8), 8)
                net = float(RATIO[c * IC + il]) * push - losses[il]
                done[rows, :] = held[rows, :] * jnp.exp(net)
            return carry

        lax.fori_loop(0, ND, one, 0, unroll=8)
        stores[c].start()
    for copy in stores:
        copy.wait()


def to_tiles(x):
    lead, rows, cols = x.shape
    x = x.reshape(lead, rows, cols // 128, 128).transpose(0, 2, 1, 3)
    return x.reshape(lead * rows * cols // 128, 128)


def from_tiles(x, shape):
    lead, rows, cols = shape
    x = x.reshape(lead, cols // 128, rows, 128).transpose(0, 2, 1, 3)
    return x.reshape(shape)


def on_device(n_strip, n_pt, spectra, courant, wind_speed, wind_dir, sea_mask, ice_mask):
    total = spectra.shape[0] * 8
    hbm = pl.BlockSpec(memory_space=pl.ANY)
    sem = pltpu.SemaphoreType.DMA
    rows = IC * ND
    whole = jax.ShapeDtypeStruct((total, 128), jnp.float32)
    point = jax.ShapeDtypeStruct((8, 128), jnp.float32)
    energy, mean_ratio, gain = pl.pallas_call(
        functools.partial(kernel, n_strip, n_pt),
        out_shape=[whole, point, jax.ShapeDtypeStruct((ND * 8, 128), jnp.float32)],
        in_specs=[hbm] * 6,
        out_specs=[hbm] * 3,
        scratch_shapes=[
            pltpu.VMEM((total, 128), jnp.float32),
            pltpu.VMEM((total, 128), jnp.float32),
            pltpu.VMEM((8, 128), jnp.int32),
            pltpu.VMEM((8, 128), jnp.float32),
            pltpu.SMEM((NF,), jnp.float32),
            pltpu.SMEM((2, NF), jnp.float32),
            pltpu.VMEM((8, 128), jnp.float32),
            pltpu.VMEM((8, 128), jnp.float32),
            pltpu.VMEM((8, 128), jnp.int32),
            pltpu.VMEM((2, CH, 2, rows, 128), jnp.float32),
            pltpu.VMEM((2, CH, 2, rows, 128), jnp.float32),
            pltpu.VMEM((2, CH, 8, 128), jnp.float32),
            pltpu.VMEM((2, CH, 2, 8, 128), jnp.float32),
            pltpu.VMEM((ND * 8, 128), jnp.float32),
            pltpu.VMEM((8, 128), jnp.float32),
            sem((CH,)),
            sem((CH,)),
            sem((5,)),
            sem((2, CH, 4)),
            sem((2, CH, 4)),
        ],
        compiler_params=pltpu.CompilerParams(
            collective_id=0, has_side_effects=True, vmem_limit_bytes=60 * 1024 * 1024
        ),
        cost_estimate=pl.CostEstimate(
            flops=30 * total * 128, bytes_accessed=8 * total * 128, transcendentals=0
        ),
    )(
        courant,
        to_tiles(sea_mask[None]),
        to_tiles(wind_speed[None]),
        to_tiles(wind_dir[None]),
        to_tiles(ice_mask[None]),
        to_tiles(spectra),
    )
    result = pl.pallas_call(
        source_kernel,
        out_shape=whole,
        in_specs=[hbm] * 4,
        out_specs=hbm,
        scratch_shapes=[
            pltpu.VMEM((total, 128), jnp.float32),
            pltpu.VMEM((total, 128), jnp.float32),
            pltpu.VMEM((ND * 8, 128), jnp.float32),
            pltpu.VMEM((8, 128), jnp.int32),
            pltpu.VMEM((8, 128), jnp.float32),
            sem((CH,)),
            sem((CH,)),
            sem((3,)),
        ],
        compiler_params=pltpu.CompilerParams(vmem_limit_bytes=60 * 1024 * 1024),
        cost_estimate=pl.CostEstimate(
            flops=4 * total * 128, bytes_accessed=8 * total * 128, transcendentals=total * 128
        ),
    )(
        gain,
        to_tiles(ice_mask[None]),
        mean_ratio,
        energy,
    )
    return from_tiles(result, spectra.shape)


def solution(mesh):
    in_specs = (
        P(None, "strip", "pt"),
        P(),
        P("strip", "pt"),
        P("strip", "pt"),
        P("strip", "pt"),
        P("strip", "pt"),
    )
    return jax.shard_map(
        functools.partial(on_device, mesh.shape["strip"], mesh.shape["pt"]),
        mesh=mesh,
        in_specs=in_specs,
        out_specs=P(None, "strip", "pt"),
        check_vma=False,
    )
```

```python
import functools
import numpy as np
import jax
import jax.numpy as jnp
from jax import lax
from jax.experimental import pallas as pl
from jax.experimental.pallas import tpu as pltpu
from jax.sharding import PartitionSpec as P

NF = 25
ND = 24
HALF = ND // 2
CH = 5
IC = NF // CH
RPI = ND * 8
RPC = RPI * IC
MESH = pl.DeviceIdType.MESH

THETA = (np.float32(2.0 * np.pi) * np.arange(ND, dtype=np.float32) / np.float32(ND)).astype(np.float32)
COS = np.cos(THETA).astype(np.float32)
SIN = np.sin(THETA).astype(np.float32)
RATIO = np.float32(1.1) ** np.arange(NF, dtype=np.float32)
WEIGHT = (RATIO / (ND * np.sum(RATIO, dtype=np.float64))).astype(np.float32)
FROM_WEST = [d for d in range(ND) if COS[d] > 0.0]
FROM_EAST = [d for d in range(ND) if not COS[d] > 0.0]


def pieces():
    return ((0, 0, 8, 0), (0, 8, 4, 8), (1, 0, 4, 12), (1, 4, 8, 16))


def kernel(
    n_strip, n_pt,
    courant_in, sea_in, wind_speed_in, wind_dir_in, ice_in, spectra,
    out, mean_out, gain_out,
    e0, e1, sea_mask, sea, courant, table, wind_speed, wind_dir, ice_mask,
    row_send, row_recv, col_send, col_recv, gain, mean,
    in_sem, out_sem, small_sem, send_sem, recv_sem,
):
    s = lax.axis_index("strip")
    p = lax.axis_index("pt")
    east = lax.rem(p + 1, n_pt)
    west = lax.rem(p + n_pt - 1, n_pt)
    has_south = s > 0
    has_north = s < n_strip - 1

    def load(c):
        rows = pl.ds(pl.multiple_of(c * RPC, RPC), RPC)
        return pltpu.make_async_copy(spectra.at[rows, :], e0.at[rows, :], in_sem.at[c])

    def store(c):
        rows = pl.ds(pl.multiple_of(c * RPC, RPC), RPC)
        return pltpu.make_async_copy(e0.at[rows, :], out.at[rows, :], out_sem.at[c])

    def rows_to(phase, c, way):
        return pltpu.make_async_remote_copy(
            src_ref=row_send.at[phase, c, way],
            dst_ref=row_recv.at[phase, c, way],
            send_sem=send_sem.at[phase, c, way],
            recv_sem=recv_sem.at[phase, c, way],
            device_id={"strip": s + 1 if way == 0 else s - 1},
            device_id_type=MESH,
        )

    def cols_to(phase, c, way):
        return pltpu.make_async_remote_copy(
            src_ref=col_send.at[phase, c],
            dst_ref=col_recv.at[phase, c, way],
            send_sem=send_sem.at[phase, c, 2 + way],
            recv_sem=recv_sem.at[phase, c, 2 + way],
            device_id={"pt": east if way == 0 else west},
            device_id_type=MESH,
        )

    def send_rows(phase, c):
        @pl.when(has_north)
        def _():
            rows_to(phase, c, 0).start()

        @pl.when(has_south)
        def _():
            rows_to(phase, c, 1).start()

    def send_cols(phase, c):
        cols_to(phase, c, 0).start()
        cols_to(phase, c, 1).start()

    def receive_rows(phase, c):
        @pl.when(has_south)
        def _():
            rows_to(phase, c, 0).wait_recv()

        @pl.when(has_north)
        def _():
            rows_to(phase, c, 1).wait_recv()

    def receive_cols(phase, c):
        cols_to(phase, c, 0).wait_recv()
        cols_to(phase, c, 1).wait_recv()

    smalls = [
        pltpu.make_async_copy(source, target, small_sem.at[n])
        for n, (source, target) in enumerate(
            (
                (courant_in, courant),
                (sea_in, sea_mask),
                (wind_speed_in, wind_speed),
                (wind_dir_in, wind_dir),
                (ice_in, ice_mask),
            )
        )
    ]
    for c in range(CH):
        load(c).start()
    for small in smalls:
        small.start()

    barrier = pltpu.get_barrier_semaphore()
    for side in (east, west):
        pl.semaphore_signal(barrier, inc=1, device_id={"pt": side}, device_id_type=MESH)

    @pl.when(has_north)
    def _():
        pl.semaphore_signal(barrier, inc=1, device_id={"strip": s + 1}, device_id_type=MESH)

    @pl.when(has_south)
    def _():
        pl.semaphore_signal(barrier, inc=1, device_id={"strip": s - 1}, device_id_type=MESH)

    @pl.when(jnp.logical_not(has_south))
    def _():
        row_recv[:, :, 0] = jnp.zeros(row_recv.shape[:2] + row_recv.shape[3:], jnp.float32)

    @pl.when(jnp.logical_not(has_north))
    def _():
        row_recv[:, :, 1] = jnp.zeros(row_recv.shape[:2] + row_recv.shape[3:], jnp.float32)

    for i in range(NF):
        table[0, i] = float(WEIGHT[i])
        table[1, i] = float(WEIGHT[i] * RATIO[i])
    lane = lax.broadcasted_iota(jnp.int32, (8, 128), 1)
    sub = lax.broadcasted_iota(jnp.int32, (8, 128), 0)
    low = sub < 4
    first_lane = lane == 0
    last_lane = lane == 127

    def pack_rows(src, phase, c):
        def one(il, carry):
            base = pl.multiple_of((c * IC + il) * RPI, 8)
            to = pl.multiple_of(il * ND, 8)
            for tile, first, count, at in pieces():
                up = src[pl.ds(base + first * 8 + 3 + 4 * tile, count, stride=8), :]
                row_send[phase, c, 0, pl.ds(to + at, count), :] = up
                down = src[pl.ds(base + (HALF + first) * 8 + 4 * tile, count, stride=8), :]
                row_send[phase, c, 1, pl.ds(to + at, count), :] = down
            return carry

        lax.fori_loop(0, IC, one, 0, unroll=True)

    spot = jnp.where(low, lane - 1, lane)

    def put(acc, n, pos, neg):
        mixed = pltpu.roll(jnp.where(low, neg, pos), n + 1, 1)
        return jnp.where(spot == n, mixed, acc)

    def pack_cols(src, phase, c):
        base = pl.multiple_of(c * RPC, 8)
        acc = jnp.zeros((8, 128), jnp.float32)
        for il in range(IC):
            for m in range(HALF):
                pos = src[pl.ds(base + il * RPI + 8 * FROM_WEST[m], 8), :]
                neg = src[pl.ds(base + il * RPI + 8 * FROM_EAST[m], 8), :]
                acc = put(acc, il * HALF + m, pos, neg)
        col_send[phase, c] = acc

    load(0).wait()
    pack_rows(e0, 0, 0)
    pl.semaphore_wait(
        barrier, 2 + has_north.astype(jnp.int32) + has_south.astype(jnp.int32)
    )
    send_rows(0, 0)
    pack_cols(e0, 0, 0)
    send_cols(0, 0)

    def first_halo(c, carry):
        load(c).wait()
        pack_rows(e0, 0, c)
        send_rows(0, c)
        pack_cols(e0, 0, c)
        send_cols(0, c)
        return carry

    lax.fori_loop(1, CH, first_halo, 0)
    for small in smalls:
        small.wait()
    sea[...] = sea_mask[...].astype(jnp.float32)

    strength = (1.0 - ice_mask[...].astype(jnp.float32)) * 0.05 * wind_speed[...]
    cos_wind = strength * jnp.cos(wind_dir[...])
    sin_wind = strength * jnp.sin(wind_dir[...])
    for d in range(ND):
        gain[pl.ds(8 * d, 8), :] = jnp.maximum(
            float(COS[d]) * cos_wind + float(SIN[d]) * sin_wind, 0.0
        )
    gain_copy = pltpu.make_async_copy(gain, gain_out, small_sem.at[0])
    gain_copy.start()

    def advance(src, dst, phase, c, sums):
        receive_cols(phase, c)
        receive_rows(phase, c)
        halo = jnp.where(low, col_recv[phase, c, 1], pltpu.roll(col_recv[phase, c, 0], 2, 1))
        halo = pltpu.roll(halo, 4, 0)
        sea_now = sea[...]
        acc = jnp.zeros((8, 128), jnp.float32)
        m0, m1 = sums
        chunk = pl.multiple_of(c * RPC, 8)
        for il in range(IC):
            i = c * IC + il
            base = chunk + il * RPI
            at = il * ND
            speed = courant[i] * sea_now
            keep = [sea_now - speed * float(k) for k in (np.abs(COS[:4]) + np.abs(SIN[:4]))]
            total = jnp.zeros((8, 128), jnp.float32)

            def step(d, core, side):
                if d < HALF:
                    near = pltpu.roll(core, 1, 0)
                    r0, r1, way, m = 0, 4, 0, d
                else:
                    near = pltpu.roll(core, 7, 0)
                    r0, r1, way, m = 3, 7, 1, d - HALF
                h0 = row_recv[phase, c, way, pl.ds(at + m, 1), :]
                h1 = row_recv[phase, c, way, pl.ds(at + HALF + m, 1), :]
                near = jnp.where(sub == r0, h0, jnp.where(sub == r1, h1, near))
                flow = float(abs(COS[d])) * side + float(abs(SIN[d])) * near
                q = d % 6
                fresh = keep[q if q < 4 else 6 - q] * core + speed * flow
                dst[pl.ds(base + 8 * d, 8), :] = fresh
                return fresh

            for m in range(HALF):
                pos = src[pl.ds(base + 8 * FROM_WEST[m], 8), :]
                neg = src[pl.ds(base + 8 * FROM_EAST[m], 8), :]
                n = il * HALF + m
                edge = pltpu.roll(halo, 126 - n, 1)
                rolled_pos = pltpu.roll(pos, 1, 1)
                rolled_neg = pltpu.roll(neg, 127, 1)
                swap = pltpu.roll(jnp.where(first_lane, rolled_pos, rolled_neg), 4, 0)
                side_pos = jnp.where(first_lane, jnp.where(low, edge, swap), rolled_pos)
                side_neg = jnp.where(last_lane, jnp.where(low, swap, edge), rolled_neg)
                new_pos = step(FROM_WEST[m], pos, side_pos)
                new_neg = step(FROM_EAST[m], neg, side_neg)
                if phase == 0:
                    acc = put(acc, n, new_pos, new_neg)
                else:
                    total = total + (new_pos + new_neg)
            if phase == 1:
                m0 = m0 + table[0, i] * total
                m1 = m1 + table[1, i] * total
        if phase == 0:
            col_send[1, c] = acc
        return m0, m1

    zero = jnp.zeros((8, 128), jnp.float32)

    def first_step(c, carry):
        advance(e0, e1, 0, c, (zero, zero))
        send_cols(1, c)
        pack_rows(e1, 1, c)
        send_rows(1, c)
        return carry

    lax.fori_loop(0, CH, first_step, 0)

    def second_step(c, sums):
        sums = advance(e1, e0, 1, c, sums)
        store(c).start()
        return sums

    m0, m1 = lax.fori_loop(0, CH, second_step, (zero, zero))
    mean[...] = m1 / jnp.maximum(m0, 0.05)
    mean_copy = pltpu.make_async_copy(mean, mean_out, small_sem.at[1])
    mean_copy.start()

    def finish(c, carry):
        for phase in range(2):
            @pl.when(has_north)
            def _():
                rows_to(phase, c, 0).wait_send()

            @pl.when(has_south)
            def _():
                rows_to(phase, c, 1).wait_send()

            cols_to(phase, c, 0).wait_send()
            cols_to(phase, c, 1).wait_send()

        store(c).wait()
        return carry

    lax.fori_loop(0, CH, finish, 0)
    gain_copy.wait()
    mean_copy.wait()


def source_kernel(
    gain_in, ice_in, mean_ratio_in, energy,
    out,
    held, done, gain, ice_mask, mean_ratio, table,
    in_sem, out_sem, small_sem,
):
    def load(c):
        rows = pl.ds(c * RPC, RPC)
        return pltpu.make_async_copy(energy.at[rows, :], held.at[rows, :], in_sem.at[c])

    def store(c):
        rows = pl.ds(c * RPC, RPC)
        return pltpu.make_async_copy(done.at[rows, :], out.at[rows, :], out_sem.at[c])

    smalls = [
        pltpu.make_async_copy(source, target, small_sem.at[n])
        for n, (source, target) in enumerate(
            (
                (mean_ratio_in, mean_ratio),
                (ice_in, ice_mask),
                (gain_in, gain),
            )
        )
    ]
    load(0).start()
    for copy in smalls:
        copy.start()
    for c in range(1, CH):
        load(c).start()
    for i in range(NF):
        table[i] = float(RATIO[i])
    for copy in smalls:
        copy.wait()
    ice = ice_mask[...].astype(jnp.float32)
    drag = 0.02 * mean_ratio[...]
    cold = 0.7 * ice

    def chunk(c, carry):
        load(c).wait()
        base = pl.multiple_of(c * RPC, 8)
        ratios = [table[c * IC + il] for il in range(IC)]
        losses = [ratio * drag + cold for ratio in ratios]
        for d in range(ND):
            push = gain[pl.ds(8 * d, 8), :]
            for il in range(IC):
                rows = pl.ds(base + il * RPI + 8 * d, 8)
                done[rows, :] = held[rows, :] * jnp.exp(ratios[il] * push - losses[il])
        store(c).start()
        return carry

    lax.fori_loop(0, CH, chunk, 0)
    for c in range(CH):
        store(c).wait()


def to_tiles(x):
    lead, rows, cols = x.shape
    x = x.reshape(lead, rows, cols // 128, 128).transpose(0, 2, 1, 3)
    return x.reshape(lead * rows * cols // 128, 128)


def from_tiles(x, shape):
    lead, rows, cols = shape
    x = x.reshape(lead, cols // 128, rows, 128).transpose(0, 2, 1, 3)
    return x.reshape(shape)


def on_device(n_strip, n_pt, spectra, courant, wind_speed, wind_dir, sea_mask, ice_mask):
    total = spectra.shape[0] * 8
    hbm = pl.BlockSpec(memory_space=pl.ANY)
    sem = pltpu.SemaphoreType.DMA
    rows = IC * ND
    whole = jax.ShapeDtypeStruct((total, 128), jnp.float32)
    point = jax.ShapeDtypeStruct((8, 128), jnp.float32)
    energy, mean_ratio, gain = pl.pallas_call(
        functools.partial(kernel, n_strip, n_pt),
        out_shape=[whole, point, jax.ShapeDtypeStruct((ND * 8, 128), jnp.float32)],
        in_specs=[hbm] * 6,
        out_specs=[hbm] * 3,
        scratch_shapes=[
            pltpu.VMEM((total, 128), jnp.float32),
            pltpu.VMEM((total, 128), jnp.float32),
            pltpu.VMEM((8, 128), jnp.int32),
            pltpu.VMEM((8, 128), jnp.float32),
            pltpu.SMEM((NF,), jnp.float32),
            pltpu.SMEM((2, NF), jnp.float32),
            pltpu.VMEM((8, 128), jnp.float32),
            pltpu.VMEM((8, 128), jnp.float32),
            pltpu.VMEM((8, 128), jnp.int32),
            pltpu.VMEM((2, CH, 2, rows, 128), jnp.float32),
            pltpu.VMEM((2, CH, 2, rows, 128), jnp.float32),
            pltpu.VMEM((2, CH, 8, 128), jnp.float32),
            pltpu.VMEM((2, CH, 2, 8, 128), jnp.float32),
            pltpu.VMEM((ND * 8, 128), jnp.float32),
            pltpu.VMEM((8, 128), jnp.float32),
            sem((CH,)),
            sem((CH,)),
            sem((5,)),
            sem((2, CH, 4)),
            sem((2, CH, 4)),
        ],
        compiler_params=pltpu.CompilerParams(
            collective_id=0, has_side_effects=True, vmem_limit_bytes=60 * 1024 * 1024
        ),
        cost_estimate=pl.CostEstimate(
            flops=30 * total * 128, bytes_accessed=8 * total * 128, transcendentals=0
        ),
    )(
        courant,
        to_tiles(sea_mask[None]),
        to_tiles(wind_speed[None]),
        to_tiles(wind_dir[None]),
        to_tiles(ice_mask[None]),
        to_tiles(spectra),
    )
    result = pl.pallas_call(
        source_kernel,
        out_shape=whole,
        in_specs=[hbm] * 4,
        out_specs=hbm,
        scratch_shapes=[
            pltpu.VMEM((total, 128), jnp.float32),
            pltpu.VMEM((total, 128), jnp.float32),
            pltpu.VMEM((ND * 8, 128), jnp.float32),
            pltpu.VMEM((8, 128), jnp.int32),
            pltpu.VMEM((8, 128), jnp.float32),
            pltpu.SMEM((NF,), jnp.float32),
            sem((CH,)),
            sem((CH,)),
            sem((3,)),
        ],
        compiler_params=pltpu.CompilerParams(vmem_limit_bytes=60 * 1024 * 1024),
        cost_estimate=pl.CostEstimate(
            flops=4 * total * 128, bytes_accessed=8 * total * 128, transcendentals=total * 128
        ),
    )(
        gain,
        to_tiles(ice_mask[None]),
        mean_ratio,
        energy,
    )
    return from_tiles(result, spectra.shape)


def solution(mesh):
    in_specs = (
        P(None, "strip", "pt"),
        P(),
        P("strip", "pt"),
        P("strip", "pt"),
        P("strip", "pt"),
        P("strip", "pt"),
    )
    return jax.shard_map(
        functools.partial(on_device, mesh.shape["strip"], mesh.shape["pt"]),
        mesh=mesh,
        in_specs=in_specs,
        out_specs=P(None, "strip", "pt"),
        check_vma=False,
    )
```

```python
import functools
import numpy as np
import jax
import jax.numpy as jnp
from jax import lax
from jax.experimental import pallas as pl
from jax.experimental.pallas import tpu as pltpu
from jax.sharding import PartitionSpec as P

NF = 25
ND = 24
HALF = ND // 2
CH = 5
IC = NF // CH
RPI = ND * 8
RPC = RPI * IC
MESH = pl.DeviceIdType.MESH

THETA = (np.float32(2.0 * np.pi) * np.arange(ND, dtype=np.float32) / np.float32(ND)).astype(np.float32)
COS = np.cos(THETA).astype(np.float32)
SIN = np.sin(THETA).astype(np.float32)
RATIO = np.float32(1.1) ** np.arange(NF, dtype=np.float32)
WEIGHT = (RATIO / (ND * np.sum(RATIO, dtype=np.float64))).astype(np.float32)
FROM_WEST = [d for d in range(ND) if COS[d] > 0.0]
FROM_EAST = [d for d in range(ND) if not COS[d] > 0.0]


def pieces():
    return ((0, 0, 8, 0), (0, 8, 4, 8), (1, 0, 4, 12), (1, 4, 8, 16))


def kernel(
    n_strip, n_pt,
    courant_in, sea_in, wind_speed_in, wind_dir_in, ice_in, spectra,
    out, mean_out, gain_out,
    e0, e1, sea_mask, sea, courant, table, wind_speed, wind_dir, ice_mask,
    row_send, row_recv, col_send, col_recv, gain, mean,
    in_sem, out_sem, small_sem, send_sem, recv_sem,
):
    s = lax.axis_index("strip")
    p = lax.axis_index("pt")
    east = lax.rem(p + 1, n_pt)
    west = lax.rem(p + n_pt - 1, n_pt)
    has_south = s > 0
    has_north = s < n_strip - 1

    def load(c):
        rows = pl.ds(pl.multiple_of(c * RPC, RPC), RPC)
        return pltpu.make_async_copy(spectra.at[rows, :], e0.at[rows, :], in_sem.at[c])

    def store(c):
        rows = pl.ds(pl.multiple_of(c * RPC, RPC), RPC)
        return pltpu.make_async_copy(e0.at[rows, :], out.at[rows, :], out_sem.at[c])

    def rows_to(phase, c, way):
        return pltpu.make_async_remote_copy(
            src_ref=row_send.at[phase, c, way],
            dst_ref=row_recv.at[phase, c, way],
            send_sem=send_sem.at[phase, c, way],
            recv_sem=recv_sem.at[phase, c, way],
            device_id={"strip": s + 1 if way == 0 else s - 1},
            device_id_type=MESH,
        )

    def cols_to(phase, c, way):
        return pltpu.make_async_remote_copy(
            src_ref=col_send.at[phase, c],
            dst_ref=col_recv.at[phase, c, way],
            send_sem=send_sem.at[phase, c, 2 + way],
            recv_sem=recv_sem.at[phase, c, 2 + way],
            device_id={"pt": east if way == 0 else west},
            device_id_type=MESH,
        )

    def send_rows(phase, c):
        @pl.when(has_south & (lax.rem(s, 2) == 0))
        def _():
            rows_to(phase, c, 1).start()

        @pl.when(has_north)
        def _():
            rows_to(phase, c, 0).start()

        @pl.when(has_south & (lax.rem(s, 2) == 1))
        def _():
            rows_to(phase, c, 1).start()

    def send_cols(phase, c):
        cols_to(phase, c, 0).start()
        cols_to(phase, c, 1).start()

    def receive_rows(phase, c):
        @pl.when(has_south)
        def _():
            rows_to(phase, c, 0).wait_recv()

        @pl.when(has_north)
        def _():
            rows_to(phase, c, 1).wait_recv()

    def receive_cols(phase, c):
        cols_to(phase, c, 0).wait_recv()
        cols_to(phase, c, 1).wait_recv()

    smalls = [
        pltpu.make_async_copy(source, target, small_sem.at[n])
        for n, (source, target) in enumerate(
            (
                (courant_in, courant),
                (sea_in, sea_mask),
                (wind_speed_in, wind_speed),
                (wind_dir_in, wind_dir),
                (ice_in, ice_mask),
            )
        )
    ]
    for c in range(CH):
        load(c).start()
    for small in smalls:
        small.start()

    barrier = pltpu.get_barrier_semaphore()
    for side in (east, west):
        pl.semaphore_signal(barrier, inc=1, device_id={"pt": side}, device_id_type=MESH)

    @pl.when(has_north)
    def _():
        pl.semaphore_signal(barrier, inc=1, device_id={"strip": s + 1}, device_id_type=MESH)

    @pl.when(has_south)
    def _():
        pl.semaphore_signal(barrier, inc=1, device_id={"strip": s - 1}, device_id_type=MESH)

    @pl.when(jnp.logical_not(has_south))
    def _():
        row_recv[:, :, 0] = jnp.zeros(row_recv.shape[:2] + row_recv.shape[3:], jnp.float32)

    @pl.when(jnp.logical_not(has_north))
    def _():
        row_recv[:, :, 1] = jnp.zeros(row_recv.shape[:2] + row_recv.shape[3:], jnp.float32)

    for i in range(NF):
        table[0, i] = float(WEIGHT[i])
        table[1, i] = float(WEIGHT[i] * RATIO[i])
    lane = lax.broadcasted_iota(jnp.int32, (8, 128), 1)
    sub = lax.broadcasted_iota(jnp.int32, (8, 128), 0)
    low = sub < 4
    first_lane = lane == 0
    last_lane = lane == 127

    def pack_rows(src, phase, c):
        def one(il, carry):
            base = pl.multiple_of((c * IC + il) * RPI, 8)
            to = pl.multiple_of(il * ND, 8)
            for tile, first, count, at in pieces():
                up = src[pl.ds(base + first * 8 + 3 + 4 * tile, count, stride=8), :]
                row_send[phase, c, 0, pl.ds(to + at, count), :] = up
                down = src[pl.ds(base + (HALF + first) * 8 + 4 * tile, count, stride=8), :]
                row_send[phase, c, 1, pl.ds(to + at, count), :] = down
            return carry

        lax.fori_loop(0, IC, one, 0, unroll=True)

    spot = jnp.where(low, lane - 1, lane)

    def put(acc, n, pos, neg):
        mixed = pltpu.roll(jnp.where(low, neg, pos), n + 1, 1)
        return jnp.where(spot == n, mixed, acc)

    def pack_cols(src, phase, c):
        base = pl.multiple_of(c * RPC, 8)
        acc = jnp.zeros((8, 128), jnp.float32)
        for il in range(IC):
            for m in range(HALF):
                pos = src[pl.ds(base + il * RPI + 8 * FROM_WEST[m], 8), :]
                neg = src[pl.ds(base + il * RPI + 8 * FROM_EAST[m], 8), :]
                acc = put(acc, il * HALF + m, pos, neg)
        col_send[phase, c] = acc

    load(0).wait()
    pack_rows(e0, 0, 0)
    pl.semaphore_wait(
        barrier, 2 + has_north.astype(jnp.int32) + has_south.astype(jnp.int32)
    )
    send_rows(0, 0)
    pack_cols(e0, 0, 0)
    send_cols(0, 0)

    def first_halo(c, carry):
        load(c).wait()
        pack_rows(e0, 0, c)
        send_rows(0, c)
        pack_cols(e0, 0, c)
        send_cols(0, c)
        return carry

    lax.fori_loop(1, CH, first_halo, 0)
    for small in smalls:
        small.wait()
    sea[...] = sea_mask[...].astype(jnp.float32)

    strength = (1.0 - ice_mask[...].astype(jnp.float32)) * 0.05 * wind_speed[...]
    cos_wind = strength * jnp.cos(wind_dir[...])
    sin_wind = strength * jnp.sin(wind_dir[...])
    for d in range(ND):
        gain[pl.ds(8 * d, 8), :] = jnp.maximum(
            float(COS[d]) * cos_wind + float(SIN[d]) * sin_wind, 0.0
        )
    gain_copy = pltpu.make_async_copy(gain, gain_out, small_sem.at[0])
    gain_copy.start()

    def advance(src, dst, phase, c, sums):
        receive_cols(phase, c)
        receive_rows(phase, c)
        halo = jnp.where(low, col_recv[phase, c, 1], pltpu.roll(col_recv[phase, c, 0], 2, 1))
        halo = pltpu.roll(halo, 4, 0)
        sea_now = sea[...]
        acc = jnp.zeros((8, 128), jnp.float32)
        m0, m1 = sums
        chunk = pl.multiple_of(c * RPC, 8)
        for il in range(IC):
            i = c * IC + il
            base = chunk + il * RPI
            at = il * ND
            speed = courant[i] * sea_now
            keep = [sea_now - speed * float(k) for k in (np.abs(COS[:4]) + np.abs(SIN[:4]))]
            total = jnp.zeros((8, 128), jnp.float32)

            def step(d, core, side):
                if d < HALF:
                    near = pltpu.roll(core, 1, 0)
                    r0, r1, way, m = 0, 4, 0, d
                else:
                    near = pltpu.roll(core, 7, 0)
                    r0, r1, way, m = 3, 7, 1, d - HALF
                h0 = row_recv[phase, c, way, pl.ds(at + m, 1), :]
                h1 = row_recv[phase, c, way, pl.ds(at + HALF + m, 1), :]
                near = jnp.where(sub == r0, h0, jnp.where(sub == r1, h1, near))
                flow = float(abs(COS[d])) * side + float(abs(SIN[d])) * near
                q = d % 6
                fresh = keep[q if q < 4 else 6 - q] * core + speed * flow
                dst[pl.ds(base + 8 * d, 8), :] = fresh
                return fresh

            for m in range(HALF):
                pos = src[pl.ds(base + 8 * FROM_WEST[m], 8), :]
                neg = src[pl.ds(base + 8 * FROM_EAST[m], 8), :]
                n = il * HALF + m
                edge = pltpu.roll(halo, 126 - n, 1)
                rolled_pos = pltpu.roll(pos, 1, 1)
                rolled_neg = pltpu.roll(neg, 127, 1)
                swap = pltpu.roll(jnp.where(first_lane, rolled_pos, rolled_neg), 4, 0)
                side_pos = jnp.where(first_lane, jnp.where(low, edge, swap), rolled_pos)
                side_neg = jnp.where(last_lane, jnp.where(low, swap, edge), rolled_neg)
                new_pos = step(FROM_WEST[m], pos, side_pos)
                new_neg = step(FROM_EAST[m], neg, side_neg)
                if phase == 0:
                    acc = put(acc, n, new_pos, new_neg)
                else:
                    total = total + (new_pos + new_neg)
            if phase == 1:
                m0 = m0 + table[0, i] * total
                m1 = m1 + table[1, i] * total
        if phase == 0:
            col_send[1, c] = acc
        return m0, m1

    zero = jnp.zeros((8, 128), jnp.float32)

    def first_step(c, carry):
        advance(e0, e1, 0, c, (zero, zero))
        send_cols(1, c)
        pack_rows(e1, 1, c)
        send_rows(1, c)
        return carry

    lax.fori_loop(0, CH, first_step, 0)

    def second_step(c, sums):
        sums = advance(e1, e0, 1, c, sums)
        store(c).start()
        return sums

    m0, m1 = lax.fori_loop(0, CH, second_step, (zero, zero))
    mean[...] = m1 / jnp.maximum(m0, 0.05)
    mean_copy = pltpu.make_async_copy(mean, mean_out, small_sem.at[1])
    mean_copy.start()

    def finish(c, carry):
        for phase in range(2):
            @pl.when(has_north)
            def _():
                rows_to(phase, c, 0).wait_send()

            @pl.when(has_south)
            def _():
                rows_to(phase, c, 1).wait_send()

            cols_to(phase, c, 0).wait_send()
            cols_to(phase, c, 1).wait_send()

        store(c).wait()
        return carry

    lax.fori_loop(0, CH, finish, 0)
    gain_copy.wait()
    mean_copy.wait()


def source_kernel(
    gain_in, ice_in, mean_ratio_in, energy,
    out,
    held, done, gain, ice_mask, mean_ratio,
    in_sem, out_sem, small_sem,
):
    loads = [
        pltpu.make_async_copy(
            energy.at[pl.ds(c * RPC, RPC), :], held.at[pl.ds(c * RPC, RPC), :], in_sem.at[c]
        )
        for c in range(CH)
    ]
    stores = [
        pltpu.make_async_copy(
            done.at[pl.ds(c * RPC, RPC), :], out.at[pl.ds(c * RPC, RPC), :], out_sem.at[c]
        )
        for c in range(CH)
    ]
    smalls = [
        pltpu.make_async_copy(source, target, small_sem.at[n])
        for n, (source, target) in enumerate(
            (
                (mean_ratio_in, mean_ratio),
                (ice_in, ice_mask),
                (gain_in, gain),
            )
        )
    ]
    for copy in smalls + loads:
        copy.start()
    for copy in smalls:
        copy.wait()
    ice = ice_mask[...].astype(jnp.float32)
    drag = 0.02 * mean_ratio[...]
    cold = 0.7 * ice
    for c in range(CH):
        loads[c].wait()
        losses = [float(RATIO[c * IC + il]) * drag + cold for il in range(IC)]

        def one(d, carry):
            push = gain[pl.ds(pl.multiple_of(8 * d, 8), 8), :]
            for il in range(IC):
                rows = pl.ds(pl.multiple_of((c * IC + il) * RPI + 8 * d, 8), 8)
                net = float(RATIO[c * IC + il]) * push - losses[il]
                done[rows, :] = held[rows, :] * jnp.exp(net)
            return carry

        lax.fori_loop(0, ND, one, 0, unroll=8)
        stores[c].start()
    for copy in stores:
        copy.wait()


def to_tiles(x):
    lead, rows, cols = x.shape
    x = x.reshape(lead, rows, cols // 128, 128).transpose(0, 2, 1, 3)
    return x.reshape(lead * rows * cols // 128, 128)


def from_tiles(x, shape):
    lead, rows, cols = shape
    x = x.reshape(lead, cols // 128, rows, 128).transpose(0, 2, 1, 3)
    return x.reshape(shape)


def on_device(n_strip, n_pt, spectra, courant, wind_speed, wind_dir, sea_mask, ice_mask):
    total = spectra.shape[0] * 8
    hbm = pl.BlockSpec(memory_space=pl.ANY)
    sem = pltpu.SemaphoreType.DMA
    rows = IC * ND
    whole = jax.ShapeDtypeStruct((total, 128), jnp.float32)
    point = jax.ShapeDtypeStruct((8, 128), jnp.float32)
    energy, mean_ratio, gain = pl.pallas_call(
        functools.partial(kernel, n_strip, n_pt),
        out_shape=[whole, point, jax.ShapeDtypeStruct((ND * 8, 128), jnp.float32)],
        in_specs=[hbm] * 6,
        out_specs=[hbm] * 3,
        scratch_shapes=[
            pltpu.VMEM((total, 128), jnp.float32),
            pltpu.VMEM((total, 128), jnp.float32),
            pltpu.VMEM((8, 128), jnp.int32),
            pltpu.VMEM((8, 128), jnp.float32),
            pltpu.SMEM((NF,), jnp.float32),
            pltpu.SMEM((2, NF), jnp.float32),
            pltpu.VMEM((8, 128), jnp.float32),
            pltpu.VMEM((8, 128), jnp.float32),
            pltpu.VMEM((8, 128), jnp.int32),
            pltpu.VMEM((2, CH, 2, rows, 128), jnp.float32),
            pltpu.VMEM((2, CH, 2, rows, 128), jnp.float32),
            pltpu.VMEM((2, CH, 8, 128), jnp.float32),
            pltpu.VMEM((2, CH, 2, 8, 128), jnp.float32),
            pltpu.VMEM((ND * 8, 128), jnp.float32),
            pltpu.VMEM((8, 128), jnp.float32),
            sem((CH,)),
            sem((CH,)),
            sem((5,)),
            sem((2, CH, 4)),
            sem((2, CH, 4)),
        ],
        compiler_params=pltpu.CompilerParams(
            collective_id=0, has_side_effects=True, vmem_limit_bytes=60 * 1024 * 1024
        ),
        cost_estimate=pl.CostEstimate(
            flops=30 * total * 128, bytes_accessed=8 * total * 128, transcendentals=0
        ),
    )(
        courant,
        to_tiles(sea_mask[None]),
        to_tiles(wind_speed[None]),
        to_tiles(wind_dir[None]),
        to_tiles(ice_mask[None]),
        to_tiles(spectra),
    )
    result = pl.pallas_call(
        source_kernel,
        out_shape=whole,
        in_specs=[hbm] * 4,
        out_specs=hbm,
        scratch_shapes=[
            pltpu.VMEM((total, 128), jnp.float32),
            pltpu.VMEM((total, 128), jnp.float32),
            pltpu.VMEM((ND * 8, 128), jnp.float32),
            pltpu.VMEM((8, 128), jnp.int32),
            pltpu.VMEM((8, 128), jnp.float32),
            sem((CH,)),
            sem((CH,)),
            sem((3,)),
        ],
        compiler_params=pltpu.CompilerParams(vmem_limit_bytes=60 * 1024 * 1024),
        cost_estimate=pl.CostEstimate(
            flops=4 * total * 128, bytes_accessed=8 * total * 128, transcendentals=total * 128
        ),
    )(
        gain,
        to_tiles(ice_mask[None]),
        mean_ratio,
        energy,
    )
    return from_tiles(result, spectra.shape)


def solution(mesh):
    in_specs = (
        P(None, "strip", "pt"),
        P(),
        P("strip", "pt"),
        P("strip", "pt"),
        P("strip", "pt"),
        P("strip", "pt"),
    )
    return jax.shard_map(
        functools.partial(on_device, mesh.shape["strip"], mesh.shape["pt"]),
        mesh=mesh,
        in_specs=in_specs,
        out_specs=P(None, "strip", "pt"),
        check_vma=False,
    )
```
